32 devices in a mesh: fsdp: 8 (over z, x), tp: 4 (over y, core).
Axes of the slice: x: 2, y: 2, z: 4, core: 2. Of those that a mesh axis runs over, the one named last changes fastest.
Arguments:
- tokens: bfloat16 [16384, 768], P(('fsdp', 'tp')), may hold values from -6 to 6
- segment_ids: int32 [16384], P('fsdp'), may hold values from 0 to 127, never falling along the last dimension, each value on 1 to 512 neighbouring positions
- query_weight: bfloat16 [768, 768], P('fsdp', 'tp'), may hold values from -0.21875 to 0.21875
- key_weight: bfloat16 [768, 768], P('fsdp', 'tp'), may hold values from -0.21875 to 0.21875
- value_weight: bfloat16 [768, 768], P('fsdp', 'tp'), may hold values from -0.21875 to 0.21875
- query_bias: float32 [768], replicated, may hold values from -3 to 3
- value_bias: float32 [768], replicated, may hold values from -3 to 3
- output_weight: bfloat16 [768, 768], P('tp', 'fsdp'), may hold values from -0.625 to 0.625
- output_bias: float32 [768], replicated, may hold values from -3 to 3
- first_gain: float32 [768], replicated, may hold values from 0.1 to 1.9
- first_shift: float32 [768], replicated, may hold values from -3 to 3
- up_weight: bfloat16 [768, 3072], P('fsdp', 'tp'), may hold values from -0.21875 to 0.21875
- up_bias: float32 [3072], replicated, may hold values from -3 to 3
- down_weight: bfloat16 [3072, 768], P('tp', 'fsdp'), may hold values from -0.109375 to 0.109375
- down_bias: float32 [768], replicated, may hold values from -3 to 3
- second_gain: float32 [768], replicated, may hold values from 0.1 to 1.9
- second_shift: float32 [768], replicated, may hold values from -3 to 3
- cotangent: bfloat16 [16384, 768], P(('fsdp', 'tp')), may hold values from -6 to 6
Outputs:
- layer_output: float32 [16384, 768], P(('fsdp', 'tp'))
- input_grad: float32 [16384, 768], P(('fsdp', 'tp'))
- query_weight_grad: float32 [768, 768], P('fsdp', 'tp')
- key_weight_grad: float32 [768, 768], P('fsdp', 'tp')
- value_weight_grad: float32 [768, 768], P('fsdp', 'tp')
- query_bias_grad: float32 [768], P('tp')
- value_bias_grad: float32 [768], P('tp')
- output_weight_grad: float32 [768, 768], P('tp', 'fsdp')
- output_bias_grad: float32 [768], replicated
- first_gain_grad: float32 [768], replicated
- first_shift_grad: float32 [768], replicated
- up_weight_grad: float32 [768, 3072], P('fsdp', 'tp')
- up_bias_grad: float32 [3072], P('tp')
- down_weight_grad: float32 [3072, 768], P('tp', 'fsdp')
- down_bias_grad: float32 [768], replicated
- second_gain_grad: float32 [768], replicated
- second_shift_grad: float32 [768], replicated
The draws below stay inside these ranges and needn't reach their ends.
Inputs may be any that keep to these rules, and one draw needn't show every extreme that they name: segment_ids never fall along the tokens; each document holds 1 to 512 tokens, and one holds exactly 512.
All inputs are finite; a program needn't handle non-finite values.
Results may differ from the reference program's by a relative error of at most 0.018.
Values may be sent and summed in bfloat16 or wider, within the bound.
No kernel may reach another device: no remote copies, remote signals or barrier semaphores. Data moves between devices by JAX's collectives and lax.ppermute only.
A program may use at most 128 MiB of HBM per device.

```python
import math
import jax
import jax.numpy as jnp
import numpy as np
from jax import lax

D = 768
H = 12
HD = 64
FF = 3072
SEQ = 512
TOKENS = 16384
N_FSDP = 8
N_TP = 4


def level_of(key, extent, pieces, smallest, largest):
    def one(axis_at, blocks):
        steps = jax.random.uniform(jax.random.fold_in(jax.random.fold_in(key, 6), axis_at), (blocks,), jnp.float32, smallest / len(pieces), largest / len(pieces))
        return jnp.repeat(jnp.exp(steps), extent[axis_at] // blocks).reshape((-1,) + (1,) * (len(extent) - axis_at - 1))

    factor_of = one(*pieces[0])
    for cut in pieces[1:]:
        factor_of = factor_of * one(*cut)
    return factor_of


def split_up(number_of, total, most, skew):
    weights = [(1 << 20) // math.isqrt(standing ** skew) + 1 for standing in range(2, number_of + 1)]
    rest, given = total - most - (number_of - 1), [1] * (number_of - 1)
    while rest > 0:
        free = [i for i in range(number_of - 1) if given[i] < most]
        whole, left = sum([weights[i] for i in free]), rest
        for i in free:
            addition = min(most - given[i], max(1, left * weights[i] // whole), rest)
            given[i] = given[i] + addition
            rest = rest - addition
    return np.array([most] + given)


def ragged_sizes(own_key, number_of, total, bound, skew):
    if number_of == 2:
        one = jax.random.randint(own_key, (), max(1, total - bound), min(bound, total - 1) + 1)
        return jnp.stack([one, total - one])
    tallies = jnp.asarray(split_up(number_of, total, bound, skew), jnp.int32)
    couples = (number_of - 1) // 2
    source_of, receiver = tallies[1:1 + 2 * couples:2], tallies[2:2 + 2 * couples:2]
    room = jnp.minimum(source_of - 1, bound - receiver)
    passed = jax.random.randint(jax.random.fold_in(own_key, 1), (couples,), 0, 1 << 20) % (room + 1)
    tallies = tallies.at[1:1 + 2 * couples:2].set(source_of - passed).at[2:2 + 2 * couples:2].set(receiver + passed)
    return tallies[jax.random.permutation(jax.random.fold_in(own_key, 2), number_of)]


def normal_values(key, shape, scale, reach, split=(), held_as=jnp.bfloat16):
    entries = scale * jax.random.normal(key, shape, jnp.float32)
    if split:
        entries = entries * level_of(key, shape, split, -0.22, 0.18)
    return jnp.clip(entries, -reach, reach).astype(held_as)


def setup_inputs(seed: int = 0) -> dict:
    key_list = jax.random.split(jax.random.key(seed), 19)
    tokens = normal_values(key_list[0], (TOKENS, D), 1.0, 6.0, ((0, 32),))
    segment_ids = jnp.searchsorted(jnp.cumsum(ragged_sizes(key_list[1], TOKENS * 4 // SEQ, TOKENS, SEQ, 1)), jnp.arange(TOKENS), side="right").astype(jnp.int32)
    query_weight = normal_values(key_list[2], (D, D), D ** -0.5, 0.21875, ((0, 8), (1, 4)))
    key_weight = normal_values(key_list[3], (D, D), D ** -0.5, 0.21875, ((0, 8), (1, 4)))
    value_weight = normal_values(key_list[4], (D, D), D ** -0.5, 0.21875, ((0, 8), (1, 4)))
    query_bias = normal_values(key_list[5], (D,), 0.5, 3.0, (), jnp.float32)
    value_bias = normal_values(key_list[6], (D,), 0.5, 3.0, (), jnp.float32)
    output_weight = normal_values(key_list[7], (D, D), (D // 8) ** -0.5, 0.625, ((0, 4), (1, 8)))
    output_bias = normal_values(key_list[8], (D,), 0.5, 3.0, (), jnp.float32)
    first_gain = jnp.clip(1.0 + 0.18 * jax.random.normal(key_list[9], (D,), jnp.float32), 0.1, 1.9)
    first_shift = normal_values(key_list[10], (D,), 0.5, 3.0, (), jnp.float32)
    up_weight = normal_values(key_list[11], (D, FF), D ** -0.5, 0.21875, ((0, 8), (1, 4)))
    up_bias = normal_values(key_list[12], (FF,), 0.5, 3.0, (), jnp.float32)
    down_weight = normal_values(key_list[13], (FF, D), FF ** -0.5, 0.109375, ((0, 4), (1, 8)))
    down_bias = normal_values(key_list[14], (D,), 0.5, 3.0, (), jnp.float32)
    second_gain = jnp.clip(1.0 + 0.18 * jax.random.normal(key_list[15], (D,), jnp.float32), 0.1, 1.9)
    second_shift = normal_values(key_list[16], (D,), 0.5, 3.0, (), jnp.float32)
    cotangent = normal_values(key_list[17], (TOKENS, D), 1.0, 6.0, ((0, 32),))
    return dict(tokens=tokens, segment_ids=segment_ids, query_weight=query_weight, key_weight=key_weight, value_weight=value_weight, query_bias=query_bias, value_bias=value_bias, output_weight=output_weight, output_bias=output_bias, first_gain=first_gain, first_shift=first_shift, up_weight=up_weight, up_bias=up_bias, down_weight=down_weight, down_bias=down_bias, second_gain=second_gain, second_shift=second_shift, cotangent=cotangent)


highest = lax.Precision.HIGHEST

@jax.custom_vjp
def low(v):
    return lax.optimization_barrier(v.astype(jnp.bfloat16)).astype(jnp.float32)

@jax.custom_vjp
def low_back(v):
    return v

def low_keep(v):
    return (low(v), None)

def low_pass(kept, grad):
    return (grad,)

def back_keep(v):
    return (v, None)

def back_low(kept, grad):
    return (low(grad),)
low.defvjp(low_keep, low_pass)
low_back.defvjp(back_keep, back_low)

def layer_norm(values, norm_gain, norm_shift):
    average = lax.optimization_barrier(jnp.mean(values, axis=-1, keepdims=True))
    centered = values - average
    variance = lax.optimization_barrier(jnp.mean(centered * centered, axis=-1, keepdims=True))
    return centered * lax.rsqrt(variance + 1e-12) * norm_gain + norm_shift

def forward(params, inputs, segments):
    query_weight, key_weight, value_weight, query_bias, value_bias, output_weight, output_bias, first_gain, first_shift, up_weight, up_bias, down_weight, down_bias, second_gain, second_shift = params
    groups = N_TP
    head_cols = D // groups
    unit_cols = FF // groups
    local_heads = H // groups
    row_count = inputs.shape[0]
    seq_count = row_count // SEQ
    copies = low_back(jnp.broadcast_to(inputs[None], (groups, row_count, D)))

    def project(weight, offset):
        result = jnp.einsum('ntd,dne->nte', copies, weight.reshape(D, groups, head_cols), precision=highest)
        return low(low_back(result + offset.reshape(groups, 1, head_cols)))

    def heads_view(tensor):
        return tensor.reshape(groups, seq_count, SEQ, local_heads, HD)
    queries = project(query_weight, query_bias)
    keys_all = project(key_weight, jnp.zeros((D,), jnp.float32))
    values_all = project(value_weight, value_bias)
    raw_scores = jnp.einsum('nsqhe,nskhe->nshqk', heads_view(queries), heads_view(keys_all), precision=highest)
    scores = low_back(raw_scores * (1.0 / math.sqrt(HD)))
    doc_ids = segments.reshape(seq_count, SEQ)
    same_doc = doc_ids[:, :, None] == doc_ids[:, None, :]
    attention = low(jax.nn.softmax(jnp.where(same_doc[None, :, None], scores, -1e+30), axis=-1))
    context = jnp.einsum('nshqk,nskhe->nsqhe', attention, heads_view(values_all), precision=highest)
    context = low(low_back(context.reshape(groups, row_count, head_cols)))
    head_parts = jnp.einsum('nte,ned->ntd', context, output_weight.reshape(groups, head_cols, D), precision=highest)
    head_parts = low(low_back(head_parts))
    first_out = layer_norm(inputs + lax.optimization_barrier(jnp.sum(head_parts, axis=0)) + output_bias, first_gain, first_shift)
    shared = low_back(jnp.broadcast_to(low(first_out)[None], (groups, row_count, D)))
    pre_act = jnp.einsum('ntd,dnf->ntf', shared, up_weight.reshape(D, groups, unit_cols), precision=highest)
    pre_act = low_back(pre_act + up_bias.reshape(groups, 1, unit_cols))
    active = low(jax.nn.gelu(pre_act, approximate=False))
    down_parts = jnp.einsum('ntf,nfd->ntd', active, down_weight.reshape(groups, unit_cols, D), precision=highest)
    down_parts = low(low_back(down_parts))
    second_in = first_out + lax.optimization_barrier(jnp.sum(down_parts, axis=0)) + down_bias
    return layer_norm(second_in, second_gain, second_shift)

def reference(tokens, segment_ids, query_weight, key_weight, value_weight, query_bias, value_bias, output_weight, output_bias, first_gain, first_shift, up_weight, up_bias, down_weight, down_bias, second_gain, second_shift, cotangent):
    params = tuple((tensor.astype(jnp.float32) for tensor in (query_weight, key_weight, value_weight, query_bias, value_bias, output_weight, output_bias, first_gain, first_shift, up_weight, up_bias, down_weight, down_bias, second_gain, second_shift)))
    group_rows = tokens.shape[0] // N_FSDP
    token_blocks = tokens.astype(jnp.float32).reshape(N_FSDP, group_rows, D)
    segment_blocks = segment_ids.reshape(N_FSDP, group_rows)
    upstream_blocks = cotangent.astype(jnp.float32).reshape(N_FSDP, group_rows, D)

    def accumulate(running, block_data):
        inputs, segments, upstream = block_data
        result, pullback = jax.vjp(lambda weights, values: forward(weights, values, segments), params, inputs)
        param_grads, input_grads = pullback(upstream)
        running = jax.tree.map(lambda former, latter: former + latter, running, param_grads)
        return (running, (result, input_grads))
    initial = jax.tree.map(jnp.zeros_like, params)
    totals, (outputs, input_grads) = lax.scan(accumulate, initial, (token_blocks, segment_blocks, upstream_blocks))
    return (outputs.reshape(-1, D), input_grads.reshape(-1, D), totals[0], totals[1], totals[2], totals[3], totals[4], totals[5], totals[6], totals[7], totals[8], totals[9], totals[10], totals[11], totals[12], totals[13], totals[14])
```

```python
from functools import partial
import math

import jax
import jax.numpy as jnp
import numpy as np
from jax import lax
from jax.experimental import pallas as pl
from jax.experimental.pallas import tpu as pltpu
from jax.sharding import PartitionSpec as P

HD = 64
SEQ = 512
AXES = ("fsdp", "tp")
F32 = jnp.float32
BF16 = jnp.bfloat16
CUTS = 8
MIB = 1 << 20


def exchange_plan(fsdp, tp):
    count = fsdp * tp
    if (fsdp, tp) == (8, 4):
        select, pairs = 1, [(8, 16), (4, 2), (16, 8), (2, 4)]
    else:
        select = tp
        pairs = [(1 << i,) * 2 for i in range(count.bit_length() - 1) if 1 << i != select]
    steps = [[d ^ pair[1 if d & select else 0] for d in range(count)] for pair in pairs]
    steps.append([d ^ select for d in range(count)])
    sources = [[d] for d in range(count)]
    for step in steps:
        sources = [sources[d] + sources[step[d]] for d in range(count)]
    return steps, np.array(sources)


def swap(array, step):
    return lax.ppermute(array, AXES, list(enumerate(step)))


def after(array, *others):
    return lax.optimization_barrier((array, *others))[0]


class Gather:
    def __init__(self, shard, steps):
        self.steps, self.at, self.held, self.pieces = steps, 0, shard[None], None

    def step(self, *others):
        step = self.steps[self.at]
        self.at += 1
        if others:
            self.held = after(self.held, *others)
        moved = swap(self.held, step)
        if self.at == len(self.steps) - 1:
            self.pieces = [self.held, moved]
        else:
            self.held = jnp.concatenate([self.held, moved], axis=0)
        return moved

    def split(self):
        parts = []
        for i in range(self.held.shape[1]):
            part = Gather(self.held[0, i], self.steps)
            part.at, part.held = self.at, self.held[:, i]
            parts.append(part)
        return parts

    def finish(self, *others):
        pieces = [after(piece, *others) for piece in self.pieces] if others else self.pieces
        return self.pieces + [swap(piece, self.steps[-1]) for piece in pieces]


class Sum:
    def __init__(self, keep, send, steps, extra=0):
        self.steps, self.at, self.keep, self.send, self.extra = steps, len(steps) - 1, keep, send, extra

    def add(self, part):
        keep, moved = self.keep[part].astype(F32), self.moved[part].astype(F32)
        if not self.extra:
            return keep + moved
        rows = keep.shape[1] - 2 * self.extra
        total = (keep + moved)[:, :rows]
        high = slice(rows, rows + self.extra)
        low = slice(rows + self.extra, None)
        side = (keep[:, high] + keep[:, low]) + (moved[:, high] + moved[:, low])
        if self.at == 0:
            return total, side
        high = lax.reduce_precision(side, 8, 7)
        return jnp.concatenate([total, high, side - high], axis=1)

    def start(self, *others):
        send = after(self.send, *others) if others else self.send
        self.moved = swap(send, self.steps[self.at])

    def end(self):
        if self.at == 0:
            return self.add(slice(None))
        half = self.keep.shape[0] // 2
        send = self.add(slice(half, None)).astype(BF16)
        keep = self.add(slice(0, half)).astype(BF16)
        self.keep, self.send = keep, send
        self.at -= 1
        return send

    def step(self, *others):
        self.start(*others)
        return self.end()

    @staticmethod
    def merge(*packages):
        one = packages[0]
        keep, send = (
            jnp.stack([getattr(package, name) for package in packages], axis=1) for name in ("keep", "send")
        )
        merged = Sum(keep, send, one.steps)
        merged.at = one.at
        return merged


def both(*packages):
    moved = lax.optimization_barrier([package.moved for package in packages])
    for package, arrived in zip(packages, moved):
        package.moved = arrived
        package.end()


def copy_block(order_ref, from_ref, to_ref):
    to_ref[...] = from_ref[...]


def laid_out(blocks, slot_of, fsdp, tp):
    _, rows, cols = blocks.shape
    grid_spec = pltpu.PrefetchScalarGridSpec(
        num_scalar_prefetch=1,
        grid=(fsdp, tp),
        in_specs=[pl.BlockSpec((1, rows, cols), lambda f, t, s: (s[f * tp + t], 0, 0))],
        out_specs=pl.BlockSpec((1, rows, cols), lambda f, t, s: (f, 0, t)),
    )
    return pl.pallas_call(
        copy_block,
        grid_spec=grid_spec,
        out_shape=jax.ShapeDtypeStruct((fsdp, rows, tp * cols), blocks.dtype),
    )(slot_of, blocks)


def cut_up(full, slot_of, fsdp, tp):
    _, rows, cols = full.shape
    cols = cols // tp
    grid_spec = pltpu.PrefetchScalarGridSpec(
        num_scalar_prefetch=1,
        grid=(fsdp, tp),
        in_specs=[pl.BlockSpec((1, rows, cols), lambda f, t, s: (f, 0, t))],
        out_specs=pl.BlockSpec((1, rows, cols), lambda f, t, s: (s[f * tp + t], 0, 0)),
    )
    return pl.pallas_call(
        copy_block,
        grid_spec=grid_spec,
        out_shape=jax.ShapeDtypeStruct((fsdp * tp, rows, cols), full.dtype),
    )(slot_of, full)


def dot(a, b):
    return lax.dot_general(a, b, (((1,), (0,)), ((), ())), preferred_element_type=F32)


def dot_nt(a, b):
    return lax.dot_general(a, b, (((1,), (1,)), ((), ())), preferred_element_type=F32)


def dot_tn(a, b):
    return lax.dot_general(a, b, (((0,), (0,)), ((), ())), preferred_element_type=F32)


def norm_forward(values):
    average = jnp.mean(values, axis=-1, keepdims=True)
    centered = values - average
    inverse = lax.rsqrt(jnp.mean(centered * centered, axis=-1, keepdims=True) + 1e-12)
    return centered * inverse, inverse


def norm_backward(upstream, normal, inverse, gain):
    scaled = upstream * gain
    return inverse * (
        scaled
        - jnp.mean(scaled, axis=-1, keepdims=True)
        - normal * jnp.mean(scaled * normal, axis=-1, keepdims=True)
    )


def gelu_parts(x):
    below = 0.5 + 0.5 * lax.erf(x * math.sqrt(0.5))
    return x * below, below + x * (jnp.exp(-0.5 * (x * x)) * (1.0 / math.sqrt(2.0 * math.pi)))


def column_sum(array):
    return jnp.sum(array, axis=0, keepdims=True)


def assemble(order_ref, pieces, weight):
    tp = weight.shape[0]
    rows = weight.shape[1] // CUTS
    per = pieces[0].shape[0]
    for i in range(per * len(pieces)):
        block = order_ref[i]
        cut = block // tp
        t = block - cut * tp
        weight[t, pl.ds(pl.multiple_of(cut * rows, rows), rows), :] = pieces[i // per][i % per]


def put_blocks(slot_ref, out_ref, tp, t, value, cols=slice(None)):
    half = out_ref.shape[0]
    rows = value.shape[0] // CUTS
    for cut in range(CUTS):
        slot = lax.rem(slot_ref[cut * tp + t], half)
        out_ref[slot, :rows, cols] = value[cut * rows : (cut + 1) * rows].astype(out_ref.dtype)


def both_halves(turn_ref, keep_ref, send_ref, tp, step):
    for half, out_ref in enumerate((keep_ref, send_ref)):
        lax.fori_loop(
            half * (tp // 2),
            (half + 1) * (tp // 2),
            lambda turn, carry, out_ref=out_ref: (step(turn_ref[turn], out_ref), carry)[1],
            0,
        )


def attention_kernel(
    pieces_n, order_ref, tokens_ref, ids_row, ids_col, bias_ref, output_bias, gain, shift, *rest,
):
    pieces, rest = rest[:pieces_n], rest[pieces_n:]
    (weight, qkv_ref, context_ref, exponent_ref, total_ref, normal_ref, inverse_ref, low_ref, turned_ref, mask,
     acc) = rest
    tp = weight.shape[0]
    cols = context_ref.shape[1]
    assemble(order_ref, pieces, weight)
    mask[...] = jnp.where(ids_col[...] == ids_row[...], 0.0, -1e30)
    acc[...] = tokens_ref[...].astype(F32) + output_bias[...]
    turned_ref[...] = tokens_ref[...].T

    def step(t, carry):
        qkv = (dot(tokens_ref[...], weight[t, :, : 3 * cols]) + bias_ref[t]).astype(BF16)
        qkv_ref[t] = qkv
        contexts = []
        for h in range(cols // HD):
            queries, keys, values = (
                qkv[:, i * cols + h * HD : i * cols + (h + 1) * HD] for i in range(3)
            )
            scores = dot_nt(keys, queries * (HD**-0.5)) + mask[...]
            top = jnp.max(scores, axis=0, keepdims=True)
            exponent = jnp.exp(scores - top)
            total = 1.0 / jnp.sum(exponent, axis=0, keepdims=True)
            exponent = exponent.astype(BF16)
            exponent_ref[t, h] = exponent
            contexts.append((dot_tn(values, exponent) * total).astype(BF16))
            total_ref[t, h : h + 1] = total
        context = jnp.concatenate(contexts, axis=0)
        context_ref[t] = context
        acc[...] += dot_nt(context.T, weight[t, :, 3 * cols :])
        return carry

    lax.fori_loop(0, tp, step, 0)
    normal, inverse = norm_forward(acc[...])
    normal_ref[...] = normal
    inverse_ref[...] = inverse
    low_ref[...] = (normal * gain[...] + shift[...]).astype(BF16)


def up_kernel(pieces_n, order_ref, low_ref, bias_ref, *rest):
    pieces, rest = rest[:pieces_n], rest[pieces_n:]
    weight, active_ref, slope_ref = rest
    tp = weight.shape[0]
    assemble(order_ref, pieces, weight)

    def step(t, carry):
        active, slope = gelu_parts(dot(low_ref[...], weight[t]) + bias_ref[t])
        active_ref[t] = active.astype(BF16)
        slope_ref[t] = slope.astype(BF16)
        return carry

    lax.fori_loop(0, tp, step, 0)


def down_kernel(
    pieces_n, order_ref, slot_ref, turn_ref, active_ref, normal_ref, first_gain, first_shift, bias_ref, gain, shift,
    cotangent_ref, *rest,
):
    pieces, rest = rest[:pieces_n], rest[pieces_n:]
    weight, output_ref, grad_ref, low_ref, sums_ref, keep_ref, send_ref, acc, turned = rest
    tp = weight.shape[0]
    assemble(order_ref, pieces, weight)
    acc[...] = normal_ref[...] * first_gain[...] + (first_shift[...] + bias_ref[...])

    def step(t, carry):
        acc[...] += dot_nt(active_ref[t], weight[t])
        return carry

    lax.fori_loop(0, tp, step, 0)
    normal, inverse = norm_forward(acc[...])
    output_ref[...] = normal * gain[...] + shift[...]
    upstream = cotangent_ref[...].astype(F32)
    grad = norm_backward(upstream, normal, inverse, gain[...])
    grad_ref[...] = grad
    low = grad.astype(BF16)
    low_ref[...] = low
    turned[...] = low.T
    sums_ref[0:1] = column_sum(grad)
    sums_ref[1:2] = column_sum(upstream * normal)
    sums_ref[2:3] = column_sum(upstream)

    def back(t, out_ref):
        put_blocks(slot_ref, out_ref, tp, t, dot(turned[...], active_ref[t]))

    both_halves(turn_ref, keep_ref, send_ref, tp, back)


def middle_kernel(
    slot_ref, turn_ref, grad_ref, low_grad_ref, low_ref, slope_ref, normal_ref, inverse_ref, gain, up_w, down_w,
    resid_ref, resid_low_ref, resid_turned_ref, sums_ref, keep_ref, send_ref, acc, turned,
):
    tp = up_w.shape[0]
    acc[...] = grad_ref[...]
    turned[...] = low_ref[...].T

    def step(t, out_ref):
        wide = dot(low_grad_ref[...], down_w[t]) * slope_ref[t].astype(F32)
        pre_grad = wide.astype(BF16)
        sums_ref[pl.ds(3 + t, 1)] = column_sum(wide)
        put_blocks(slot_ref, out_ref, tp, t, dot(turned[...], pre_grad))
        acc[...] += dot_nt(pre_grad, up_w[t])

    both_halves(turn_ref, keep_ref, send_ref, tp, step)
    grad_one = acc[...]
    normal = normal_ref[...]
    resid = norm_backward(grad_one, normal, inverse_ref[...], gain[...])
    resid_ref[...] = resid
    low = resid.astype(BF16)
    resid_low_ref[...] = low
    resid_turned_ref[...] = low.T
    sums_ref[0:1] = column_sum(resid)
    sums_ref[1:2] = column_sum(grad_one * normal)
    sums_ref[2:3] = column_sum(grad_one)


def attention_back_kernel(
    slot_ref, turn_ref, turned_ref, qkv_ref, context_ref, exponent_ref, total_ref, resid_ref, resid_low_ref,
    resid_turned_ref, sums_in_ref, weight, grad_ref, sums_ref, keep_ref, send_ref,
):
    tp = weight.shape[0]
    cols = context_ref.shape[1]
    grad_ref[...] = resid_ref[...]
    factor = HD**-0.5
    extra = sums_ref.shape[1]
    main = keep_ref.shape[1] - 2 * extra
    half = keep_ref.shape[0]

    def step(t, out_ref):
        outer = dot(resid_low_ref[...], weight[t, :, 3 * cols :])
        totals = total_ref[t].T
        query_grads, key_grads, value_grads = [], [], []
        for h in range(cols // HD):
            at = slice(h * HD, (h + 1) * HD)
            queries, keys, values = (
                qkv_ref[t, :, i * cols + h * HD : i * cols + (h + 1) * HD] for i in range(3)
            )
            queries = queries * factor
            upstream = (outer[:, at] * totals[:, h : h + 1]).astype(BF16)
            row_term = jnp.sum(
                upstream.T.astype(F32) * context_ref[t, at].astype(F32), axis=0, keepdims=True
            )
            exponent = exponent_ref[t, h]
            prob_grad = dot_nt(values, upstream)
            score_grad = (exponent.astype(F32) * (prob_grad - row_term)).astype(BF16)
            key_grads.append(dot(score_grad, queries).astype(BF16))
            value_grads.append(dot(exponent, upstream).astype(BF16))
            query_grads.append((dot_tn(keys, score_grad) * factor).astype(BF16))
        queries = jnp.concatenate(query_grads, axis=0).T
        grad = jnp.concatenate([queries, *key_grads, *value_grads], axis=1)
        grad_ref[...] += dot_nt(grad, weight[t, :, : 3 * cols])
        put_blocks(slot_ref, out_ref, tp, t, dot(turned_ref[...], grad), slice(0, 3 * cols))
        out_grad = dot_nt(resid_turned_ref[...], context_ref[t])
        put_blocks(slot_ref, out_ref, tp, t, out_grad, slice(3 * cols, None))
        columns = column_sum(grad.astype(F32))
        side = jnp.concatenate([columns, jnp.zeros((1, cols), F32)], axis=1)
        side = jnp.concatenate([sums_in_ref[t], side], axis=0)
        sums_ref[t] = side
        high = side.astype(BF16)
        low = (side - high.astype(F32)).astype(BF16)
        side = jnp.concatenate([high, low], axis=0)
        for cut in range(CUTS):
            out_ref[lax.rem(slot_ref[cut * tp + t], half), main:, :] = side

    both_halves(turn_ref, keep_ref, send_ref, tp, step)


def call(kernel, pieces, scalars, inputs, outs, scratch, flops, limit=22):
    whole = pl.BlockSpec(memory_space=pltpu.VMEM)
    smem = pl.BlockSpec(memory_space=pltpu.SMEM)
    return pl.pallas_call(
        kernel,
        in_specs=[smem] * len(scalars) + [whole] * len(inputs) + [whole] * len(pieces),
        out_specs=[whole] * len(outs),
        out_shape=[jax.ShapeDtypeStruct(*out) for out in outs],
        scratch_shapes=scratch,
        compiler_params=pltpu.CompilerParams(vmem_limit_bytes=limit * MIB),
        cost_estimate=pl.CostEstimate(flops=flops, bytes_accessed=16 * MIB, transcendentals=0),
    )(*scalars, *inputs, *pieces)


def shards(
    steps,
    sources,
    fsdp,
    tp,
    tokens,
    segment_ids,
    query_weight,
    key_weight,
    value_weight,
    query_bias,
    value_bias,
    output_weight,
    output_bias,
    first_gain,
    first_shift,
    up_weight,
    up_bias,
    down_weight,
    down_bias,
    second_gain,
    second_shift,
    cotangent,
):
    rows, cols = query_weight.shape
    width = rows * fsdp
    units = up_weight.shape[1]
    count = fsdp * tp
    cut_rows = width // CUTS
    blocks_n = CUTS * tp
    direct = blocks_n == count
    place = lax.axis_index("tp")
    me = lax.axis_index("fsdp") * tp + place
    doc_ids = lax.dynamic_slice_in_dim(segment_ids, place * SEQ, SEQ)

    def mine(table):
        return lax.dynamic_index_in_dim(jnp.asarray(table, jnp.int32), me, keepdims=False)

    slot_of = mine(np.argsort(sources, axis=1))
    if direct:
        order, slots = mine(sources), slot_of
        turns = mine(np.argsort(np.argsort(sources, axis=1)[:, :tp] // (count // 2), axis=1, kind="stable"))
    else:
        cut, t = np.divmod(np.arange(blocks_n), tp)
        kept = tp // 2
        order = jnp.arange(blocks_n, dtype=jnp.int32)
        slots = jnp.asarray(t // kept * (CUTS * kept) + cut * kept + t % kept, jnp.int32)
        turns = jnp.arange(tp, dtype=jnp.int32)

    def ready(pieces):
        if direct:
            return pieces
        full = laid_out(jnp.concatenate(pieces, axis=0), slot_of, fsdp, tp)
        full = full.reshape(CUTS, cut_rows, tp, -1).transpose(0, 2, 1, 3)
        return [full.reshape(blocks_n, cut_rows, -1)]

    def outgoing(keep, send, extra=0):
        if direct:
            return Sum(keep, send, steps, extra)
        blocks = jnp.concatenate([keep, send], axis=0)[:, :cut_rows]
        full = blocks.reshape(2, CUTS, tp // 2, cut_rows, -1).transpose(1, 3, 0, 2, 4)
        blocks = cut_up(full.reshape(fsdp, rows, -1), slot_of, fsdp, tp)
        return Sum(blocks[: count // 2], blocks[count // 2 :], steps)

    query_bias, value_bias = query_bias.reshape(tp, 1, cols), value_bias.reshape(tp, 1, cols)
    blank = jnp.zeros_like(query_bias)
    qkv_bias = jnp.concatenate([query_bias, blank, value_bias], axis=2)
    up_bias = up_bias.reshape(tp, 1, units)
    vectors = jnp.stack(
        [output_bias, first_gain, first_shift, down_bias, second_gain, second_shift]
    ).reshape(6, 1, width)
    output_bias, first_gain, first_shift, down_bias, second_gain, second_shift = (
        vectors[i] for i in range(6)
    )
    ids_row, ids_col = doc_ids.reshape(1, -1), doc_ids.reshape(-1, 1)

    a = Gather(jnp.concatenate([query_weight, key_weight, value_weight, output_weight.T], axis=1), steps)
    b = Gather(up_weight, steps)
    c = Gather(down_weight.T, steps)
    if direct:
        pair = Gather(jnp.stack([up_weight, down_weight.T]), steps)
        first = a.step()
        pair.held = after(pair.held, first)
        a_x = a.step(qkv_bias, up_bias, vectors, ids_row, ids_col)
        pair.step()
        a.held, pair.held = lax.optimization_barrier((a.held, pair.held))
        a.step()
        pair.step()
        a.held, pair.held = lax.optimization_barrier((a.held, pair.held))
        b, c = pair.split()
        a_x = a.step()
        b_z = b.step()
        a.pieces, b.held = lax.optimization_barrier((a.pieces, b.held))
        attn_w = ready(a.finish())
        b_x = b.step()
        c_z = c.step(b_z)
    else:
        for package in (a, b, c):
            for _ in steps[:-1]:
                package.step()
        attn_w = ready(a.finish())
    pieces_n = len(attn_w)

    weight = ((tp, width, units), BF16)
    state = pltpu.VMEM((SEQ, width), F32)
    turned = pltpu.VMEM((width, SEQ), BF16)
    mask = pltpu.VMEM((SEQ, SEQ), F32)
    wide = (SEQ, width)
    flops = 2 * SEQ * width * width
    attn_full, qkv, context, exponent, total, normal, inverse, low, tokens_turned = call(
        partial(attention_kernel, pieces_n),
        attn_w,
        (order,),
        (tokens, ids_row, ids_col, qkv_bias, output_bias, first_gain, first_shift),
        [weight, ((tp, SEQ, 3 * cols), BF16), ((tp, cols, SEQ), BF16),
         ((tp, cols // HD, SEQ, SEQ), BF16), ((tp, 8, SEQ), F32), (wide, F32),
         ((SEQ, 1), F32), (wide, BF16), ((width, SEQ), BF16)],
        [mask, state],
        8 * flops,
    )
    if direct:
        up_w = b.finish(inverse)
        c.step(inverse, b_x)
    else:
        up_w = ready(b.finish())
    up_full, active, slope = call(
        partial(up_kernel, pieces_n),
        up_w,
        (order,),
        (low, up_bias),
        [weight, ((tp, SEQ, units), BF16), ((tp, SEQ, units), BF16)],
        [],
        5 * flops,
    )
    down_w = c.finish(slope) if direct else ready(c.finish())
    half = ((blocks_n // 2, cut_rows, units), BF16)
    down_full, layer_output, grad_two, grad_low, down_sums, *down_blocks = call(
        partial(down_kernel, pieces_n),
        down_w,
        (order, slots, turns),
        (active, normal, first_gain, first_shift, down_bias, second_gain, second_shift, cotangent),
        [weight, (wide, F32), (wide, F32), (wide, BF16), ((8, width), F32), half, half],
        [state, turned],
        10 * flops,
    )
    down_sum = outgoing(*down_blocks)
    if direct:
        first = down_sum.step()
        down_sum.start()
        grad_low = after(grad_low, first)
    resid, resid_low, resid_turned, middle_sums, *up_blocks = call(
        middle_kernel,
        [up_full, down_full],
        (slots, turns),
        (grad_two, grad_low, low, slope, normal, inverse, first_gain),
        [(wide, F32), (wide, BF16), ((width, SEQ), BF16), ((8, width), F32), half, half],
        [state, turned],
        12 * flops,
    )
    up_sum = outgoing(*up_blocks)
    if direct:
        moved = down_sum.moved
        sent = down_sum.end()
        down_sum.start(middle_sums)
        first = up_sum.step(moved)
        up_sum.start()
        resid_low = after(resid_low, first, sent)
    sides = jnp.broadcast_to(jnp.concatenate([down_sums[:3], middle_sums[:3]], axis=0), (tp, 6, width))
    sides = jnp.concatenate([sides, middle_sums[3 : 3 + tp, None]], axis=1)
    part = ((blocks_n // 2, cut_rows + 16, units), BF16)
    input_grad, side, *attn_blocks = call(
        attention_back_kernel,
        [attn_full],
        (slots, turns),
        (tokens_turned, qkv, context, exponent, total, resid, resid_low, resid_turned, sides),
        [(wide, F32), ((tp, 8, units), F32), part, part],
        [],
        20 * flops,
    )
    attn_sum = outgoing(*attn_blocks, 8)
    if direct:
        attn_sum.step(down_sum.moved, up_sum.moved)
        down_sum.end()
        up_sum.end()
        attn_sum.start()
        up_sum.start()
        both(attn_sum, up_sum)
        pair = Sum.merge(down_sum, up_sum)
        attn_sum.start()
        pair.start()
        both(attn_sum, pair)
        attn_sum.start()
        pair.start()
        attn_sum.end()
        finals = [[part] for part in pair.end()[0]]
        attn_sum.start()
        finals.append(attn_sum.end())
    else:
        finals = []
        for package in (down_sum, up_sum, attn_sum):
            while package.at > 0:
                package.step()
            package.start()
            finals.append(package.end())
    if direct:
        attn_grad, side = finals[2][0][0], finals[2][1][0]
    else:
        attn_grad = finals[2][0]
        side = lax.dynamic_index_in_dim(lax.psum(side, AXES), place, keepdims=False)
    return (
        layer_output,
        input_grad,
        attn_grad[:, :cols],
        attn_grad[:, cols : 2 * cols],
        attn_grad[:, 2 * cols : 3 * cols],
        side[7, :cols],
        side[7, 2 * cols : 3 * cols],
        attn_grad[:, 3 * cols :].T,
        side[3],
        side[4],
        side[5],
        finals[1][0],
        side[6],
        finals[0][0].T,
        side[0],
        side[1],
        side[2],
    )


def solution(mesh):
    fsdp, tp = mesh.shape["fsdp"], mesh.shape["tp"]
    steps, sources = exchange_plan(fsdp, tp)
    both, up, down = P(AXES, None), P("fsdp", "tp"), P("tp", "fsdp")
    return jax.shard_map(
        partial(shards, steps, sources, fsdp, tp),
        mesh=mesh,
        in_specs=(
            both, P("fsdp"), up, up, up, P(), P(), down, P(), P(), P(), up, P(), down, P(), P(), P(), both,
        ),
        out_specs=(
            both, both, up, up, up, P("tp"), P("tp"), down, P(), P(), P(), up, P("tp"), down, P(), P(), P(),
        ),
        check_vma=False,
    )
```

```python
from functools import partial
import math

import jax
import jax.numpy as jnp
import numpy as np
from jax import lax
from jax.experimental import pallas as pl
from jax.experimental.pallas import tpu as pltpu
from jax.sharding import PartitionSpec as P

HD = 64
SEQ = 512
AXES = ("fsdp", "tp")
F32 = jnp.float32
BF16 = jnp.bfloat16
CUTS = 8
MIB = 1 << 20


def exchange_plan(fsdp, tp):
    count = fsdp * tp
    if (fsdp, tp) == (8, 4):
        select, pairs = 1, [(8, 16), (4, 2), (16, 8), (2, 4)]
    else:
        select = tp
        pairs = [(1 << i,) * 2 for i in range(count.bit_length() - 1) if 1 << i != select]
    steps = [[d ^ pair[1 if d & select else 0] for d in range(count)] for pair in pairs]
    steps.append([d ^ select for d in range(count)])
    sources = [[d] for d in range(count)]
    for step in steps:
        sources = [sources[d] + sources[step[d]] for d in range(count)]
    return steps, np.array(sources)


def swap(array, step):
    return lax.ppermute(array, AXES, list(enumerate(step)))


def after(array, *others):
    return lax.optimization_barrier((array, *others))[0]


class Gather:
    def __init__(self, shard, steps):
        self.steps, self.at, self.held, self.pieces = steps, 0, shard[None], None

    def step(self, *others):
        step = self.steps[self.at]
        self.at += 1
        if others:
            self.held = after(self.held, *others)
        moved = swap(self.held, step)
        if self.at == len(self.steps) - 1:
            self.pieces = [self.held, moved]
        else:
            self.held = jnp.concatenate([self.held, moved], axis=0)
        return moved

    def split(self):
        parts = []
        for i in range(self.held.shape[1]):
            part = Gather(self.held[0, i], self.steps)
            part.at, part.held = self.at, self.held[:, i]
            parts.append(part)
        return parts

    def finish(self, *others):
        pieces = [after(piece, *others) for piece in self.pieces] if others else self.pieces
        return self.pieces + [swap(piece, self.steps[-1]) for piece in pieces]


class Sum:
    def __init__(self, keep, send, steps, extra=0):
        self.steps, self.at, self.keep, self.send, self.extra = steps, len(steps) - 1, keep, send, extra

    def add(self, keep, moved):
        keep, moved = keep.astype(F32), moved.astype(F32)
        if not self.extra:
            return keep + moved
        rows = keep.shape[1] - 2 * self.extra
        total = (keep + moved)[:, :rows]
        high = slice(rows, rows + self.extra)
        low = slice(rows + self.extra, None)
        side = (keep[:, high] + keep[:, low]) + (moved[:, high] + moved[:, low])
        if self.at == 0:
            return total, side
        high = lax.reduce_precision(side, 8, 7)
        return jnp.concatenate([total, high, side - high], axis=1)

    def start(self, *others):
        send = after(self.send, *others) if others else self.send
        half = send.shape[0] // 2
        parts = [send[:half], send[half:]] if self.at == len(self.steps) - 1 else [send]
        self.moved = [swap(part, self.steps[self.at]) for part in parts]

    def hold(self, *others):
        self.moved = list(lax.optimization_barrier((*self.moved, *others))[: len(self.moved)])

    def end(self):
        if self.at == 0:
            return self.add(self.keep, self.moved[0])
        half = self.keep.shape[0] // 2
        if len(self.moved) == 1:
            moved = self.moved[0][:half], self.moved[0][half:]
        else:
            moved = self.moved
        send = self.add(self.keep[half:], moved[1]).astype(BF16)
        keep = self.add(self.keep[:half], moved[0]).astype(BF16)
        self.keep, self.send = keep, send
        self.at -= 1
        return send

    def step(self, *others):
        self.start(*others)
        return self.end()

    @staticmethod
    def merge(*packages):
        one = packages[0]
        keep, send = (
            jnp.stack([getattr(package, name) for package in packages], axis=1) for name in ("keep", "send")
        )
        merged = Sum(keep, send, one.steps)
        merged.at = one.at
        return merged


def both(*packages):
    moved = lax.optimization_barrier([package.moved for package in packages])
    for package, arrived in zip(packages, moved):
        package.moved = arrived
        package.end()


def copy_block(order_ref, from_ref, to_ref):
    to_ref[...] = from_ref[...]


def laid_out(blocks, slot_of, fsdp, tp):
    _, rows, cols = blocks.shape
    grid_spec = pltpu.PrefetchScalarGridSpec(
        num_scalar_prefetch=1,
        grid=(fsdp, tp),
        in_specs=[pl.BlockSpec((1, rows, cols), lambda f, t, s: (s[f * tp + t], 0, 0))],
        out_specs=pl.BlockSpec((1, rows, cols), lambda f, t, s: (f, 0, t)),
    )
    return pl.pallas_call(
        copy_block,
        grid_spec=grid_spec,
        out_shape=jax.ShapeDtypeStruct((fsdp, rows, tp * cols), blocks.dtype),
    )(slot_of, blocks)


def cut_up(full, slot_of, fsdp, tp):
    _, rows, cols = full.shape
    cols = cols // tp
    grid_spec = pltpu.PrefetchScalarGridSpec(
        num_scalar_prefetch=1,
        grid=(fsdp, tp),
        in_specs=[pl.BlockSpec((1, rows, cols), lambda f, t, s: (f, 0, t))],
        out_specs=pl.BlockSpec((1, rows, cols), lambda f, t, s: (s[f * tp + t], 0, 0)),
    )
    return pl.pallas_call(
        copy_block,
        grid_spec=grid_spec,
        out_shape=jax.ShapeDtypeStruct((fsdp * tp, rows, cols), full.dtype),
    )(slot_of, full)


def dot(a, b):
    return lax.dot_general(a, b, (((1,), (0,)), ((), ())), preferred_element_type=F32)


def dot_nt(a, b):
    return lax.dot_general(a, b, (((1,), (1,)), ((), ())), preferred_element_type=F32)


def dot_tn(a, b):
    return lax.dot_general(a, b, (((0,), (0,)), ((), ())), preferred_element_type=F32)


def norm_forward(values):
    average = jnp.mean(values, axis=-1, keepdims=True)
    centered = values - average
    inverse = lax.rsqrt(jnp.mean(centered * centered, axis=-1, keepdims=True) + 1e-12)
    return centered * inverse, inverse


def norm_backward(upstream, normal, inverse, gain):
    scaled = upstream * gain
    return inverse * (
        scaled
        - jnp.mean(scaled, axis=-1, keepdims=True)
        - normal * jnp.mean(scaled * normal, axis=-1, keepdims=True)
    )


def gelu_parts(x):
    below = 0.5 + 0.5 * lax.erf(x * math.sqrt(0.5))
    return x * below, below + x * (jnp.exp(-0.5 * (x * x)) * (1.0 / math.sqrt(2.0 * math.pi)))


def column_sum(array):
    return jnp.sum(array, axis=0, keepdims=True)


def assemble(half, place_ref, pieces, weight):
    rows = weight.shape[1] // CUTS
    per = pieces[0].shape[0]
    count = per * len(pieces)
    for slot in range(count):
        place = place_ref[half * count + slot]
        i = place // CUTS
        cut = place - i * CUTS
        weight[i, pl.ds(pl.multiple_of(cut * rows, rows), rows), :] = pieces[slot // per][slot % per]


def put_blocks(half, slot_ref, out_ref, i, value, cols=slice(None)):
    rows = value.shape[0] // CUTS
    for cut in range(CUTS):
        slot = slot_ref[half * out_ref.shape[0] + i * CUTS + cut]
        out_ref[slot, :rows, cols] = value[cut * rows : (cut + 1) * rows].astype(out_ref.dtype)


def each(count, step):
    lax.fori_loop(0, count, lambda i, carry: (step(i), carry)[1], 0)


def attention_kernel(half, place_ref, turn_ref, tokens_ref, ids_row, ids_col, bias_ref, *rest):
    if half == 0:
        output_bias, *rest = rest
        *pieces, weight, qkv_ref, context_ref, exponent_ref, total_ref, acc, turned_ref, mask = rest
        acc[...] = tokens_ref[...].astype(F32) + output_bias[...]
        turned_ref[...] = tokens_ref[...].T
    else:
        acc_ref, gain, shift, *rest = rest
        *pieces, weight, qkv_ref, context_ref, exponent_ref, total_ref = rest[:-5]
        normal_ref, inverse_ref, low_ref, mask, acc = rest[-5:]
        acc[...] = acc_ref[...]
    cols = context_ref.shape[1]
    count = weight.shape[0]
    assemble(half, place_ref, pieces, weight)
    mask[...] = jnp.where(ids_col[...] == ids_row[...], 0.0, -1e30)

    def step(i):
        bias = bias_ref[turn_ref[half * count + i]]
        qkv = (dot(tokens_ref[...], weight[i, :, : 3 * cols]) + bias).astype(BF16)
        qkv_ref[i] = qkv
        contexts = []
        for h in range(cols // HD):
            queries, keys, values = (
                qkv[:, part * cols + h * HD : part * cols + (h + 1) * HD] for part in range(3)
            )
            scores = dot_nt(keys, queries * (HD**-0.5)) + mask[...]
            top = jnp.max(scores, axis=0, keepdims=True)
            exponent = jnp.exp(scores - top)
            total = 1.0 / jnp.sum(exponent, axis=0, keepdims=True)
            exponent = exponent.astype(BF16)
            exponent_ref[i, h] = exponent
            contexts.append((dot_tn(values, exponent) * total).astype(BF16))
            total_ref[i, h : h + 1] = total
        context = jnp.concatenate(contexts, axis=0)
        context_ref[i] = context
        acc[...] += dot_nt(context.T, weight[i, :, 3 * cols :])

    each(count, step)
    if half == 1:
        normal, inverse = norm_forward(acc[...])
        normal_ref[...] = normal
        inverse_ref[...] = inverse
        low_ref[...] = (normal * gain[...] + shift[...]).astype(BF16)


def up_kernel(place_ref, turn_ref, low_ref, bias_ref, *rest):
    *pieces, weight_first, active_first, slope_first, weight_second, active_second, slope_second = rest
    many = len(pieces) // 2
    up_half(0, place_ref, turn_ref, low_ref, bias_ref, pieces[:many], weight_first, active_first, slope_first)
    up_half(1, place_ref, turn_ref, low_ref, bias_ref, pieces[many:], weight_second, active_second, slope_second)


def up_half(half, place_ref, turn_ref, low_ref, bias_ref, pieces, weight, active_ref, slope_ref):
    count = weight.shape[0]
    assemble(half, place_ref, pieces, weight)

    def step(i):
        pre = dot(low_ref[...], weight[i]) + bias_ref[turn_ref[half * count + i]]
        active, slope = gelu_parts(pre)
        active_ref[i] = active.astype(BF16)
        slope_ref[i] = slope.astype(BF16)

    each(count, step)


def down_first_kernel(place_ref, active_ref, normal_ref, first_gain, first_shift, bias_ref, *rest):
    *pieces, weight, acc = rest
    assemble(0, place_ref, pieces, weight)
    acc[...] = normal_ref[...] * first_gain[...] + (first_shift[...] + bias_ref[...])

    def step(i):
        acc[...] += dot_nt(active_ref[i], weight[i])

    each(weight.shape[0], step)


def down_second_kernel(place_ref, slot_ref, active_ref, acc_ref, gain, shift, cotangent_ref, *rest):
    *pieces, weight, output_ref, grad_ref, low_ref, turned_ref, sums_ref, send_ref, acc = rest
    count = weight.shape[0]
    assemble(1, place_ref, pieces, weight)
    acc[...] = acc_ref[...]

    def step(i):
        acc[...] += dot_nt(active_ref[i], weight[i])

    each(count, step)
    normal, inverse = norm_forward(acc[...])
    output_ref[...] = normal * gain[...] + shift[...]
    upstream = cotangent_ref[...].astype(F32)
    grad = norm_backward(upstream, normal, inverse, gain[...])
    grad_ref[...] = grad
    low = grad.astype(BF16)
    low_ref[...] = low
    turned_ref[...] = low.T
    sums_ref[0:1] = column_sum(grad)
    sums_ref[1:2] = column_sum(upstream * normal)
    sums_ref[2:3] = column_sum(upstream)
    each(count, lambda i: put_blocks(1, slot_ref, send_ref, i, dot(turned_ref[...], active_ref[i])))


def down_third_kernel(slot_ref, active_ref, turned_ref, keep_ref):
    each(
        active_ref.shape[0],
        lambda i: put_blocks(0, slot_ref, keep_ref, i, dot(turned_ref[...], active_ref[i])),
    )


def middle_kernel(half, slot_ref, low_grad_ref, slope_ref, *rest):
    if half == 1:
        grad_ref, low_ref, up_w, down_w, out_ref, sums_ref, acc, turned = rest
        acc[...] = grad_ref[...]
        turned[...] = low_ref[...].T
    else:
        acc_ref, turned, normal_ref, inverse_ref, gain, up_w, down_w, *rest = rest
        out_ref, sums_ref, resid_ref, resid_low_ref, resid_turned_ref, acc = rest
        acc[...] = acc_ref[...]

    def step(i):
        wide = dot(low_grad_ref[...], down_w[i]) * slope_ref[i].astype(F32)
        pre_grad = wide.astype(BF16)
        sums_ref[pl.ds(3 + i, 1)] = column_sum(wide)
        put_blocks(half, slot_ref, out_ref, i, dot(turned[...], pre_grad))
        acc[...] += dot_nt(pre_grad, up_w[i])

    each(up_w.shape[0], step)
    if half == 0:
        grad_one = acc[...]
        normal = normal_ref[...]
        resid = norm_backward(grad_one, normal, inverse_ref[...], gain[...])
        resid_ref[...] = resid
        low = resid.astype(BF16)
        resid_low_ref[...] = low
        resid_turned_ref[...] = low.T
        sums_ref[0:1] = column_sum(resid)
        sums_ref[1:2] = column_sum(grad_one * normal)
        sums_ref[2:3] = column_sum(grad_one)


def attention_back_kernel(slot_ref, turned_ref, resid_ref, resid_low_ref, resid_turned_ref, *rest):
    *parts, grad_ref, sums_second, sums_first, send_ref, keep_ref = rest
    grad_ref[...] = resid_ref[...]
    many = len(parts) // 2
    shared = (slot_ref, turned_ref, resid_low_ref, resid_turned_ref, grad_ref)
    attention_back(1, *shared, *parts[:many], sums_second, send_ref)
    attention_back(0, *shared, *parts[many:], sums_first, keep_ref)


def attention_back(
    half, slot_ref, turned_ref, resid_low_ref, resid_turned_ref, grad_ref, sums_in_ref, qkv_ref, context_ref,
    exponent_ref, total_ref, weight, sums_ref, out_ref,
):
    cols = context_ref.shape[1]
    factor = HD**-0.5
    extra = sums_ref.shape[1]
    main = out_ref.shape[1] - 2 * extra

    def step(i):
        outer = dot(resid_low_ref[...], weight[i, :, 3 * cols :])
        totals = total_ref[i].T
        query_grads, key_grads, value_grads = [], [], []
        for h in range(cols // HD):
            at = slice(h * HD, (h + 1) * HD)
            queries, keys, values = (
                qkv_ref[i, :, part * cols + h * HD : part * cols + (h + 1) * HD] for part in range(3)
            )
            queries = queries * factor
            upstream = (outer[:, at] * totals[:, h : h + 1]).astype(BF16)
            row_term = jnp.sum(
                upstream.T.astype(F32) * context_ref[i, at].astype(F32), axis=0, keepdims=True
            )
            exponent = exponent_ref[i, h]
            prob_grad = dot_nt(values, upstream)
            score_grad = (exponent.astype(F32) * (prob_grad - row_term)).astype(BF16)
            key_grads.append(dot(score_grad, queries).astype(BF16))
            value_grads.append(dot(exponent, upstream).astype(BF16))
            query_grads.append((dot_tn(keys, score_grad) * factor).astype(BF16))
        queries = jnp.concatenate(query_grads, axis=0).T
        grad = jnp.concatenate([queries, *key_grads, *value_grads], axis=1)
        grad_ref[...] += dot_nt(grad, weight[i, :, : 3 * cols])
        put_blocks(half, slot_ref, out_ref, i, dot(turned_ref[...], grad), slice(0, 3 * cols))
        out_grad = dot_nt(resid_turned_ref[...], context_ref[i])
        put_blocks(half, slot_ref, out_ref, i, out_grad, slice(3 * cols, None))
        columns = column_sum(grad.astype(F32))
        side = jnp.concatenate([columns, jnp.zeros((1, cols), F32)], axis=1)
        side = jnp.concatenate([sums_in_ref[i], side], axis=0)
        sums_ref[i] = side
        high = side.astype(BF16)
        low = (side - high.astype(F32)).astype(BF16)
        side = jnp.concatenate([high, low], axis=0)
        for cut in range(CUTS):
            out_ref[slot_ref[half * out_ref.shape[0] + i * CUTS + cut], main:, :] = side

    each(weight.shape[0], step)


def call(kernel, pieces, scalars, inputs, outs, scratch, flops, limit=16):
    whole = pl.BlockSpec(memory_space=pltpu.VMEM)
    smem = pl.BlockSpec(memory_space=pltpu.SMEM)
    return pl.pallas_call(
        kernel,
        in_specs=[smem] * len(scalars) + [whole] * len(inputs) + [whole] * len(pieces),
        out_specs=[whole] * len(outs),
        out_shape=[jax.ShapeDtypeStruct(*out) for out in outs],
        scratch_shapes=scratch,
        compiler_params=pltpu.CompilerParams(vmem_limit_bytes=limit * MIB),
        cost_estimate=pl.CostEstimate(flops=1024, bytes_accessed=1024, transcendentals=0),
    )(*scalars, *inputs, *pieces)


def shards(
    steps,
    sources,
    fsdp,
    tp,
    tokens,
    segment_ids,
    query_weight,
    key_weight,
    value_weight,
    query_bias,
    value_bias,
    output_weight,
    output_bias,
    first_gain,
    first_shift,
    up_weight,
    up_bias,
    down_weight,
    down_bias,
    second_gain,
    second_shift,
    cotangent,
):
    rows, cols = query_weight.shape
    width = rows * fsdp
    units = up_weight.shape[1]
    count = fsdp * tp
    cut_rows = width // CUTS
    blocks_n = CUTS * tp
    direct = blocks_n == count
    place = lax.axis_index("tp")
    me = lax.axis_index("fsdp") * tp + place
    doc_ids = lax.dynamic_slice_in_dim(segment_ids, place * SEQ, SEQ)

    def mine(table):
        return lax.dynamic_index_in_dim(jnp.asarray(table, jnp.int32), me, keepdims=False)

    slot_of = mine(np.argsort(sources, axis=1))
    kept = tp // 2
    if direct:
        sides = np.array(sources).reshape(count, 2, -1) % tp
        columns = np.sort(np.array([[np.unique(part) for part in parts] for parts in sides]), axis=2)
        inner = (sides[..., None] == columns[:, :, None, :]).argmax(axis=-1)
        spots = inner * CUTS + np.array(sources).reshape(count, 2, -1) // tp
        places = mine(spots.reshape(count, -1))
        slots = mine(np.argsort(spots, axis=2).reshape(count, -1))
        turns = mine(columns.reshape(count, -1))
    else:
        places = slots = jnp.tile(jnp.arange(blocks_n // 2, dtype=jnp.int32), 2)
        turns = jnp.arange(tp, dtype=jnp.int32)

    def ready(pieces):
        if direct:
            return pieces
        full = laid_out(jnp.concatenate(pieces, axis=0), slot_of, fsdp, tp)
        full = full.reshape(CUTS, cut_rows, tp, -1).transpose(2, 0, 1, 3)
        full = full.reshape(2, blocks_n // 2, cut_rows, -1)
        return [full[0], full[1]]

    def outgoing(keep, send, extra=0):
        if direct:
            return Sum(keep, send, steps, extra)
        blocks = jnp.concatenate([keep, send], axis=0)[:, :cut_rows]
        full = blocks.reshape(tp, CUTS, cut_rows, -1).transpose(1, 2, 0, 3)
        blocks = cut_up(full.reshape(fsdp, rows, -1), slot_of, fsdp, tp)
        return Sum(blocks[: count // 2], blocks[count // 2 :], steps)

    query_bias, value_bias = query_bias.reshape(tp, 1, cols), value_bias.reshape(tp, 1, cols)
    blank = jnp.zeros_like(query_bias)
    qkv_bias = jnp.concatenate([query_bias, blank, value_bias], axis=2)
    up_bias = up_bias.reshape(tp, 1, units)
    vectors = jnp.stack(
        [output_bias, first_gain, first_shift, down_bias, second_gain, second_shift]
    ).reshape(6, 1, width)
    output_bias, first_gain, first_shift, down_bias, second_gain, second_shift = (
        vectors[i] for i in range(6)
    )
    ids_row, ids_col = doc_ids.reshape(1, -1), doc_ids.reshape(-1, 1)

    a = Gather(jnp.concatenate([query_weight, key_weight, value_weight, output_weight.T], axis=1), steps)
    b = Gather(up_weight, steps)
    c = Gather(down_weight.T, steps)
    if direct:
        pair = Gather(jnp.stack([up_weight, down_weight.T]), steps)
        first = a.step()
        pair.held = after(pair.held, first)
        a_x = a.step(qkv_bias, up_bias, vectors, ids_row, ids_col)
        pair.step()
        a.held, pair.held = lax.optimization_barrier((a.held, pair.held))
        a.step()
        pair.step()
        a.held, pair.held = lax.optimization_barrier((a.held, pair.held))
        b, c = pair.split()
        a_x = a.step()
        b_z = b.step()
        a.pieces, b.held = lax.optimization_barrier((a.pieces, b.held))
        attn_w = ready(a.finish())
        b_x = b.step()
        c_z = c.step(b_z)
    else:
        for package in (a, b, c):
            for _ in steps[:-1]:
                package.step()
        attn_w = ready(a.finish())
    many = len(attn_w) // 2
    parts = kept
    weight = ((parts, width, units), BF16)
    half = ((blocks_n // 2, cut_rows, units), BF16)
    side_half = ((blocks_n // 2, cut_rows + 16, units), BF16)
    state = pltpu.VMEM((SEQ, width), F32)
    turned = pltpu.VMEM((width, SEQ), BF16)
    mask = pltpu.VMEM((SEQ, SEQ), F32)
    wide, narrow = (SEQ, width), ((SEQ, width), BF16)
    full = (wide, F32)
    flipped = ((width, SEQ), BF16)
    flops = 2 * SEQ * width * width
    kept_outs = [weight, ((parts, SEQ, 3 * cols), BF16), ((parts, cols, SEQ), BF16),
                 ((parts, cols // HD, SEQ, SEQ), BF16), ((parts, 8, SEQ), F32)]
    common = (tokens, ids_row, ids_col, qkv_bias)
    *attn_first, acc, tokens_turned = call(
        partial(attention_kernel, 0), attn_w[:many], (places, turns), (*common, output_bias),
        [*kept_outs, full, flipped], [mask], 4 * flops,
    )
    *attn_second, normal, inverse, low = call(
        partial(attention_kernel, 1), attn_w[many:], (places, turns), (*common, acc, first_gain, first_shift),
        [*kept_outs, full, ((SEQ, 1), F32), narrow], [mask, state], 4 * flops,
    )
    if direct:
        up_w = b.finish(inverse)
        c.step(inverse, b_x)
    else:
        up_w = ready(b.finish())
    outs = [weight, ((parts, SEQ, units), BF16), ((parts, SEQ, units), BF16)]
    up_first, active_first, slope_first, up_second, active_second, slope_second = call(
        up_kernel, up_w, (places, turns), (low, up_bias), outs * 2, [], 6 * flops
    )
    down_w = c.finish(slope_second) if direct else ready(c.finish())
    down_first, acc = call(
        down_first_kernel, down_w[:many], (places,),
        (active_first, normal, first_gain, first_shift, down_bias), [weight, full], [], 2 * flops,
    )
    down_second, layer_output, grad_two, grad_low, grad_turned, down_sums, down_send = call(
        down_second_kernel, down_w[many:], (places, slots),
        (active_second, acc, second_gain, second_shift, cotangent),
        [weight, full, full, narrow, flipped, ((8, width), F32), half], [state], 5 * flops,
    )
    (down_keep,) = call(
        down_third_kernel, [], (slots,), (active_first, grad_turned), [half], [], 2 * flops
    )
    down_sum = outgoing(down_keep, down_send)
    if direct:
        first = down_sum.step()
        down_sum.start()
        grad_low = after(grad_low, first)
    up_send, sums_second, acc, low_turned = call(
        partial(middle_kernel, 1), [up_second, down_second], (slots,),
        (grad_low, slope_second, grad_two, low), [half, ((8, width), F32), full, flipped], [], 6 * flops,
    )
    up_keep, sums_first, resid, resid_low, resid_turned = call(
        partial(middle_kernel, 0), [up_first, down_first], (slots,),
        (grad_low, slope_first, acc, low_turned, normal, inverse, first_gain),
        [half, ((8, width), F32), full, narrow, flipped], [state], 6 * flops,
    )
    up_sum = outgoing(up_keep, up_send)
    if direct:
        moved = down_sum.moved
        sent = down_sum.end()
        down_sum.start(sums_first)
        up_sum.start()
        up_sum.hold(resid_low, sent)
        first = up_sum.end()
        up_sum.start()
        resid_low = after(resid_low, first, sent)
    shared = jnp.concatenate([down_sums[:3], sums_first[:3]], axis=0)[None]

    def with_units(sums):
        return jnp.concatenate([jnp.broadcast_to(shared, (parts, 6, width)), sums[3 : 3 + parts, None]], axis=1)

    weight_second, *attn_second = attn_second
    weight_first, *attn_first = attn_first
    side_sums = ((parts, 8, units), F32)
    input_grad, side_second, side_first, attn_send, attn_keep = call(
        attention_back_kernel, [], (slots,),
        (tokens_turned, resid, resid_low, resid_turned, with_units(sums_second), *attn_second, weight_second,
         with_units(sums_first), *attn_first, weight_first),
        [full, side_sums, side_sums, side_half, side_half], [], 20 * flops,
    )
    attn_sum = outgoing(attn_keep, attn_send, 8)
    if direct:
        attn_sum.step(*down_sum.moved, *up_sum.moved)
        down_sum.end()
        up_sum.end()
        attn_sum.start()
        up_sum.start()
        both(attn_sum, up_sum)
        pair = Sum.merge(down_sum, up_sum)
        attn_sum.start()
        pair.start()
        both(attn_sum, pair)
        attn_sum.start()
        pair.start()
        attn_sum.end()
        finals = [[part] for part in pair.end()[0]]
        attn_sum.start()
        finals.append(attn_sum.end())
    else:
        side = jnp.concatenate([side_first, side_second], axis=0)
        finals = []
        for package in (down_sum, up_sum, attn_sum):
            while package.at > 0:
                package.step()
            package.start()
            finals.append(package.end())
    if direct:
        attn_grad, side = finals[2][0][0], finals[2][1][0]
    else:
        attn_grad = finals[2][0]
        side = lax.dynamic_index_in_dim(lax.psum(side, AXES), place, keepdims=False)
    return (
        layer_output,
        input_grad,
        attn_grad[:, :cols],
        attn_grad[:, cols : 2 * cols],
        attn_grad[:, 2 * cols : 3 * cols],
        side[7, :cols],
        side[7, 2 * cols : 3 * cols],
        attn_grad[:, 3 * cols :].T,
        side[3],
        side[4],
        side[5],
        finals[1][0],
        side[6],
        finals[0][0].T,
        side[0],
        side[1],
        side[2],
    )


def solution(mesh):
    fsdp, tp = mesh.shape["fsdp"], mesh.shape["tp"]
    steps, sources = exchange_plan(fsdp, tp)
    both, up, down = P(AXES, None), P("fsdp", "tp"), P("tp", "fsdp")
    return jax.shard_map(
        partial(shards, steps, sources, fsdp, tp),
        mesh=mesh,
        in_specs=(
            both, P("fsdp"), up, up, up, P(), P(), down, P(), P(), P(), up, P(), down, P(), P(), P(), both,
        ),
        out_specs=(
            both, both, up, up, up, P("tp"), P("tp"), down, P(), P(), P(), up, P("tp"), down, P(), P(), P(),
        ),
        check_vma=False,
    )
```

```python
from functools import partial
import math

import jax
import jax.numpy as jnp
import numpy as np
from jax import lax
from jax.experimental import pallas as pl
from jax.experimental.pallas import tpu as pltpu
from jax.sharding import PartitionSpec as P

HD = 64
SEQ = 512
AXES = ("fsdp", "tp")
F32 = jnp.float32
BF16 = jnp.bfloat16
CUTS = 8
MIB = 1 << 20


def exchange_plan(fsdp, tp):
    count = fsdp * tp
    if (fsdp, tp) == (8, 4):
        select, pairs = 1, [(8, 16), (4, 2), (16, 8), (2, 4)]
    else:
        select = tp
        pairs = [(1 << i,) * 2 for i in range(count.bit_length() - 1) if 1 << i != select]
    steps = [[d ^ pair[1 if d & select else 0] for d in range(count)] for pair in pairs]
    steps.append([d ^ select for d in range(count)])
    sources = [[d] for d in range(count)]
    for step in steps:
        sources = [sources[d] + sources[step[d]] for d in range(count)]
    return steps, np.array(sources)


def swap(array, step):
    return lax.ppermute(array, AXES, list(enumerate(step)))


def after(array, *others):
    return lax.optimization_barrier((array, *others))[0]


class Gather:
    def __init__(self, shard, steps):
        self.steps, self.at, self.held, self.pieces = steps, 0, shard[None], None

    def step(self, *others):
        step = self.steps[self.at]
        self.at += 1
        if others:
            self.held = after(self.held, *others)
        moved = swap(self.held, step)
        if self.at == len(self.steps) - 1:
            self.pieces = [self.held, moved]
        else:
            self.held = jnp.concatenate([self.held, moved], axis=0)
        return moved

    def split(self):
        parts = []
        for i in range(self.held.shape[1]):
            part = Gather(self.held[0, i], self.steps)
            part.at, part.held = self.at, self.held[:, i]
            parts.append(part)
        return parts

    def finish(self, *others):
        pieces = [after(piece, *others) for piece in self.pieces] if others else self.pieces
        return self.pieces + [swap(piece, self.steps[-1]) for piece in pieces]


class Sum:
    def __init__(self, keep, send, steps, extra=0):
        self.steps, self.at, self.keep, self.send, self.extra = steps, len(steps) - 1, keep, send, extra

    def add(self, keep, moved):
        keep, moved = keep.astype(F32), moved.astype(F32)
        if not self.extra:
            return keep + moved
        rows = keep.shape[1] - 2 * self.extra
        total = (keep + moved)[:, :rows]
        high = slice(rows, rows + self.extra)
        low = slice(rows + self.extra, None)
        side = (keep[:, high] + keep[:, low]) + (moved[:, high] + moved[:, low])
        if self.at == 0:
            return total, side
        high = lax.reduce_precision(side, 8, 7)
        return jnp.concatenate([total, high, side - high], axis=1)

    def start(self, *others):
        send = after(self.send, *others) if others else self.send
        half = send.shape[0] // 2
        parts = [send[:half], send[half:]] if self.at == len(self.steps) - 1 else [send]
        self.moved = [swap(part, self.steps[self.at]) for part in parts]

    def hold(self, *others):
        self.moved = list(lax.optimization_barrier((*self.moved, *others))[: len(self.moved)])

    def end(self):
        if self.at == 0:
            return self.add(self.keep, self.moved[0])
        half = self.keep.shape[0] // 2
        if len(self.moved) == 1:
            moved = self.moved[0][:half], self.moved[0][half:]
        else:
            moved = self.moved
        send = self.add(self.keep[half:], moved[1]).astype(BF16)
        keep = self.add(self.keep[:half], moved[0]).astype(BF16)
        self.keep, self.send = keep, send
        self.at -= 1
        return send

    def step(self, *others):
        self.start(*others)
        return self.end()

    @staticmethod
    def merge(*packages):
        one = packages[0]
        keep, send = (
            jnp.stack([getattr(package, name) for package in packages], axis=1) for name in ("keep", "send")
        )
        merged = Sum(keep, send, one.steps)
        merged.at = one.at
        return merged


def both(*packages):
    moved = lax.optimization_barrier([package.moved for package in packages])
    for package, arrived in zip(packages, moved):
        package.moved = arrived
        package.end()


def copy_block(order_ref, from_ref, to_ref):
    to_ref[...] = from_ref[...]


def laid_out(blocks, slot_of, fsdp, tp):
    _, rows, cols = blocks.shape
    grid_spec = pltpu.PrefetchScalarGridSpec(
        num_scalar_prefetch=1,
        grid=(fsdp, tp),
        in_specs=[pl.BlockSpec((1, rows, cols), lambda f, t, s: (s[f * tp + t], 0, 0))],
        out_specs=pl.BlockSpec((1, rows, cols), lambda f, t, s: (f, 0, t)),
    )
    return pl.pallas_call(
        copy_block,
        grid_spec=grid_spec,
        out_shape=jax.ShapeDtypeStruct((fsdp, rows, tp * cols), blocks.dtype),
    )(slot_of, blocks)


def cut_up(full, slot_of, fsdp, tp):
    _, rows, cols = full.shape
    cols = cols // tp
    grid_spec = pltpu.PrefetchScalarGridSpec(
        num_scalar_prefetch=1,
        grid=(fsdp, tp),
        in_specs=[pl.BlockSpec((1, rows, cols), lambda f, t, s: (f, 0, t))],
        out_specs=pl.BlockSpec((1, rows, cols), lambda f, t, s: (s[f * tp + t], 0, 0)),
    )
    return pl.pallas_call(
        copy_block,
        grid_spec=grid_spec,
        out_shape=jax.ShapeDtypeStruct((fsdp * tp, rows, cols), full.dtype),
    )(slot_of, full)


def dot(a, b):
    return lax.dot_general(a, b, (((1,), (0,)), ((), ())), preferred_element_type=F32)


def dot_nt(a, b):
    return lax.dot_general(a, b, (((1,), (1,)), ((), ())), preferred_element_type=F32)


def dot_tn(a, b):
    return lax.dot_general(a, b, (((0,), (0,)), ((), ())), preferred_element_type=F32)


def norm_forward(values):
    average = jnp.mean(values, axis=-1, keepdims=True)
    centered = values - average
    inverse = lax.rsqrt(jnp.mean(centered * centered, axis=-1, keepdims=True) + 1e-12)
    return centered * inverse, inverse


def norm_backward(upstream, normal, inverse, gain):
    scaled = upstream * gain
    return inverse * (
        scaled
        - jnp.mean(scaled, axis=-1, keepdims=True)
        - normal * jnp.mean(scaled * normal, axis=-1, keepdims=True)
    )


def gelu_parts(x):
    below = 0.5 + 0.5 * lax.erf(x * math.sqrt(0.5))
    return x * below, below + x * (jnp.exp(-0.5 * (x * x)) * (1.0 / math.sqrt(2.0 * math.pi)))


def column_sum(array):
    return jnp.sum(array, axis=0, keepdims=True)


def assemble(half, place_ref, pieces, weight):
    rows = weight.shape[1] // CUTS
    per = pieces[0].shape[0]
    count = per * len(pieces)
    for slot in range(count):
        place = place_ref[half * count + slot]
        i = place // CUTS
        cut = place - i * CUTS
        weight[i, pl.ds(pl.multiple_of(cut * rows, rows), rows), :] = pieces[slot // per][slot % per]


def put_blocks(half, slot_ref, out_ref, i, value, cols=slice(None)):
    rows = value.shape[0] // CUTS
    for cut in range(CUTS):
        slot = slot_ref[half * out_ref.shape[0] + i * CUTS + cut]
        out_ref[slot, :rows, cols] = value[cut * rows : (cut + 1) * rows].astype(out_ref.dtype)


def each(count, step):
    for i in range(count):
        step(i)


def attention_kernel(half, place_ref, turn_ref, tokens_ref, ids_row, ids_col, bias_ref, *rest):
    if half == 0:
        output_bias, *rest = rest
        *pieces, weight, qkv_ref, context_ref, exponent_ref, total_ref, acc, turned_ref, mask = rest
        acc[...] = tokens_ref[...].astype(F32) + output_bias[...]
        turned_ref[...] = tokens_ref[...].T
    else:
        acc_ref, gain, shift, *rest = rest
        *pieces, weight, qkv_ref, context_ref, exponent_ref, total_ref = rest[:-5]
        normal_ref, inverse_ref, low_ref, mask, acc = rest[-5:]
        acc[...] = acc_ref[...]
    cols = context_ref.shape[1]
    count = weight.shape[0]
    assemble(half, place_ref, pieces, weight)
    mask[...] = jnp.where(ids_col[...] == ids_row[...], 0.0, -1e30)

    def step(i):
        bias = bias_ref[turn_ref[half * count + i]]
        qkv = (dot(tokens_ref[...], weight[i, :, : 3 * cols]) + bias).astype(BF16)
        qkv_ref[i] = qkv
        contexts = []
        for h in range(cols // HD):
            queries, keys, values = (
                qkv[:, part * cols + h * HD : part * cols + (h + 1) * HD] for part in range(3)
            )
            scores = dot_nt(keys, queries * (HD**-0.5)) + mask[...]
            top = jnp.max(scores, axis=0, keepdims=True)
            exponent = jnp.exp(scores - top)
            total = 1.0 / jnp.sum(exponent, axis=0, keepdims=True)
            exponent = exponent.astype(BF16)
            exponent_ref[i, h] = exponent
            contexts.append((dot_tn(values, exponent) * total).astype(BF16))
            total_ref[i, h : h + 1] = total
        context = jnp.concatenate(contexts, axis=0)
        context_ref[i] = context
        acc[...] += dot_nt(context.T, weight[i, :, 3 * cols :])

    each(count, step)
    if half == 1:
        normal, inverse = norm_forward(acc[...])
        normal_ref[...] = normal
        inverse_ref[...] = inverse
        low_ref[...] = (normal * gain[...] + shift[...]).astype(BF16)


def up_kernel(place_ref, turn_ref, low_ref, bias_ref, *rest):
    *pieces, weight_first, active_first, slope_first, weight_second, active_second, slope_second = rest
    many = len(pieces) // 2
    up_half(0, place_ref, turn_ref, low_ref, bias_ref, pieces[:many], weight_first, active_first, slope_first)
    up_half(1, place_ref, turn_ref, low_ref, bias_ref, pieces[many:], weight_second, active_second, slope_second)


def up_half(half, place_ref, turn_ref, low_ref, bias_ref, pieces, weight, active_ref, slope_ref):
    count = weight.shape[0]
    assemble(half, place_ref, pieces, weight)

    def step(i):
        pre = dot(low_ref[...], weight[i]) + bias_ref[turn_ref[half * count + i]]
        active, slope = gelu_parts(pre)
        active_ref[i] = active.astype(BF16)
        slope_ref[i] = slope.astype(BF16)

    each(count, step)


def down_first_kernel(place_ref, active_ref, normal_ref, first_gain, first_shift, bias_ref, *rest):
    *pieces, weight, acc = rest
    assemble(0, place_ref, pieces, weight)
    acc[...] = normal_ref[...] * first_gain[...] + (first_shift[...] + bias_ref[...])

    def step(i):
        acc[...] += dot_nt(active_ref[i], weight[i])

    each(weight.shape[0], step)


def down_second_kernel(place_ref, slot_ref, active_ref, acc_ref, gain, shift, cotangent_ref, *rest):
    *pieces, weight, output_ref, grad_ref, low_ref, turned_ref, sums_ref, send_ref, acc = rest
    count = weight.shape[0]
    assemble(1, place_ref, pieces, weight)
    acc[...] = acc_ref[...]

    def step(i):
        acc[...] += dot_nt(active_ref[i], weight[i])

    each(count, step)
    normal, inverse = norm_forward(acc[...])
    output_ref[...] = normal * gain[...] + shift[...]
    upstream = cotangent_ref[...].astype(F32)
    grad = norm_backward(upstream, normal, inverse, gain[...])
    grad_ref[...] = grad
    low = grad.astype(BF16)
    low_ref[...] = low
    turned_ref[...] = low.T
    sums_ref[0:1] = column_sum(grad)
    sums_ref[1:2] = column_sum(upstream * normal)
    sums_ref[2:3] = column_sum(upstream)
    each(count, lambda i: put_blocks(1, slot_ref, send_ref, i, dot(turned_ref[...], active_ref[i])))


def down_third_kernel(slot_ref, active_ref, turned_ref, keep_ref):
    each(
        active_ref.shape[0],
        lambda i: put_blocks(0, slot_ref, keep_ref, i, dot(turned_ref[...], active_ref[i])),
    )


def middle_kernel(half, slot_ref, low_grad_ref, slope_ref, *rest):
    if half == 1:
        grad_ref, low_ref, up_w, down_w, out_ref, sums_ref, acc, turned = rest
        acc[...] = grad_ref[...]
        turned[...] = low_ref[...].T
    else:
        acc_ref, turned, normal_ref, inverse_ref, gain, up_w, down_w, *rest = rest
        out_ref, sums_ref, resid_ref, resid_low_ref, resid_turned_ref, acc = rest
        acc[...] = acc_ref[...]

    def step(i):
        wide = dot(low_grad_ref[...], down_w[i]) * slope_ref[i].astype(F32)
        pre_grad = wide.astype(BF16)
        sums_ref[pl.ds(3 + i, 1)] = column_sum(wide)
        put_blocks(half, slot_ref, out_ref, i, dot(turned[...], pre_grad))
        acc[...] += dot_nt(pre_grad, up_w[i])

    each(up_w.shape[0], step)
    if half == 0:
        grad_one = acc[...]
        normal = normal_ref[...]
        resid = norm_backward(grad_one, normal, inverse_ref[...], gain[...])
        resid_ref[...] = resid
        low = resid.astype(BF16)
        resid_low_ref[...] = low
        resid_turned_ref[...] = low.T
        sums_ref[0:1] = column_sum(resid)
        sums_ref[1:2] = column_sum(grad_one * normal)
        sums_ref[2:3] = column_sum(grad_one)


def attention_back_kernel(slot_ref, turned_ref, resid_ref, resid_low_ref, resid_turned_ref, *rest):
    *parts, grad_ref, sums_second, sums_first, send_ref, keep_ref = rest
    grad_ref[...] = resid_ref[...]
    many = len(parts) // 2
    shared = (slot_ref, turned_ref, resid_low_ref, resid_turned_ref, grad_ref)
    attention_back(1, *shared, *parts[:many], sums_second, send_ref)
    attention_back(0, *shared, *parts[many:], sums_first, keep_ref)


def attention_back(
    half, slot_ref, turned_ref, resid_low_ref, resid_turned_ref, grad_ref, sums_in_ref, qkv_ref, context_ref,
    exponent_ref, total_ref, weight, sums_ref, out_ref,
):
    cols = context_ref.shape[1]
    factor = HD**-0.5
    extra = sums_ref.shape[1]
    main = out_ref.shape[1] - 2 * extra
    grads = []

    def step(i):
        outer = dot(resid_low_ref[...], weight[i, :, 3 * cols :])
        totals = total_ref[i].T
        query_grads, key_grads, value_grads = [], [], []
        for h in range(cols // HD):
            at = slice(h * HD, (h + 1) * HD)
            queries, keys, values = (
                qkv_ref[i, :, part * cols + h * HD : part * cols + (h + 1) * HD] for part in range(3)
            )
            queries = queries * factor
            upstream = (outer[:, at] * totals[:, h : h + 1]).astype(BF16)
            row_term = jnp.sum(
                upstream.T.astype(F32) * context_ref[i, at].astype(F32), axis=0, keepdims=True
            )
            exponent = exponent_ref[i, h]
            prob_grad = dot_nt(values, upstream)
            score_grad = (exponent.astype(F32) * (prob_grad - row_term)).astype(BF16)
            key_grads.append(dot(score_grad, queries).astype(BF16))
            value_grads.append(dot(exponent, upstream).astype(BF16))
            query_grads.append((dot_tn(keys, score_grad) * factor).astype(BF16))
        queries = jnp.concatenate(query_grads, axis=0).T
        grads.append(jnp.concatenate([queries, *key_grads, *value_grads], axis=1))

    each(weight.shape[0], step)
    count = weight.shape[0]
    grad = jnp.concatenate(grads, axis=1)
    grad_ref[...] += dot_nt(grad, jnp.concatenate([weight[i, :, : 3 * cols] for i in range(count)], axis=1))
    weight_grad = dot(turned_ref[...], grad)
    out_grad = dot_nt(resid_turned_ref[...], jnp.concatenate([context_ref[i] for i in range(count)], axis=0))
    columns = column_sum(grad.astype(F32))
    for i in range(count):
        put_blocks(half, slot_ref, out_ref, i, weight_grad[:, 3 * cols * i : 3 * cols * (i + 1)], slice(0, 3 * cols))
        put_blocks(half, slot_ref, out_ref, i, out_grad[:, cols * i : cols * (i + 1)], slice(3 * cols, None))
        side = jnp.concatenate([columns[:, 3 * cols * i : 3 * cols * (i + 1)], jnp.zeros((1, cols), F32)], axis=1)
        side = jnp.concatenate([sums_in_ref[i], side], axis=0)
        sums_ref[i] = side
        high = side.astype(BF16)
        low = (side - high.astype(F32)).astype(BF16)
        side = jnp.concatenate([high, low], axis=0)
        for cut in range(CUTS):
            out_ref[slot_ref[half * out_ref.shape[0] + i * CUTS + cut], main:, :] = side


def call(kernel, pieces, scalars, inputs, outs, scratch, flops, limit=16):
    whole = pl.BlockSpec(memory_space=pltpu.VMEM)
    smem = pl.BlockSpec(memory_space=pltpu.SMEM)
    return pl.pallas_call(
        kernel,
        in_specs=[smem] * len(scalars) + [whole] * len(inputs) + [whole] * len(pieces),
        out_specs=[whole] * len(outs),
        out_shape=[jax.ShapeDtypeStruct(*out) for out in outs],
        scratch_shapes=scratch,
        compiler_params=pltpu.CompilerParams(vmem_limit_bytes=limit * MIB),
        cost_estimate=pl.CostEstimate(flops=1024, bytes_accessed=1024, transcendentals=0),
    )(*scalars, *inputs, *pieces)


def shards(
    steps,
    sources,
    fsdp,
    tp,
    tokens,
    segment_ids,
    query_weight,
    key_weight,
    value_weight,
    query_bias,
    value_bias,
    output_weight,
    output_bias,
    first_gain,
    first_shift,
    up_weight,
    up_bias,
    down_weight,
    down_bias,
    second_gain,
    second_shift,
    cotangent,
):
    rows, cols = query_weight.shape
    width = rows * fsdp
    units = up_weight.shape[1]
    count = fsdp * tp
    cut_rows = width // CUTS
    blocks_n = CUTS * tp
    direct = blocks_n == count
    place = lax.axis_index("tp")
    me = lax.axis_index("fsdp") * tp + place
    doc_ids = lax.dynamic_slice_in_dim(segment_ids, place * SEQ, SEQ)

    def mine(table):
        return lax.dynamic_index_in_dim(jnp.asarray(table, jnp.int32), me, keepdims=False)

    slot_of = mine(np.argsort(sources, axis=1))
    kept = tp // 2
    if direct:
        sides = np.array(sources).reshape(count, 2, -1) % tp
        columns = np.sort(np.array([[np.unique(part) for part in parts] for parts in sides]), axis=2)
        inner = (sides[..., None] == columns[:, :, None, :]).argmax(axis=-1)
        spots = inner * CUTS + np.array(sources).reshape(count, 2, -1) // tp
        places = mine(spots.reshape(count, -1))
        slots = mine(np.argsort(spots, axis=2).reshape(count, -1))
        turns = mine(columns.reshape(count, -1))
    else:
        places = slots = jnp.tile(jnp.arange(blocks_n // 2, dtype=jnp.int32), 2)
        turns = jnp.arange(tp, dtype=jnp.int32)

    def ready(pieces):
        if direct:
            return pieces
        full = laid_out(jnp.concatenate(pieces, axis=0), slot_of, fsdp, tp)
        full = full.reshape(CUTS, cut_rows, tp, -1).transpose(2, 0, 1, 3)
        full = full.reshape(2, blocks_n // 2, cut_rows, -1)
        return [full[0], full[1]]

    def outgoing(keep, send, extra=0):
        if direct:
            return Sum(keep, send, steps, extra)
        blocks = jnp.concatenate([keep, send], axis=0)[:, :cut_rows]
        full = blocks.reshape(tp, CUTS, cut_rows, -1).transpose(1, 2, 0, 3)
        blocks = cut_up(full.reshape(fsdp, rows, -1), slot_of, fsdp, tp)
        return Sum(blocks[: count // 2], blocks[count // 2 :], steps)

    query_bias, value_bias = query_bias.reshape(tp, 1, cols), value_bias.reshape(tp, 1, cols)
    blank = jnp.zeros_like(query_bias)
    qkv_bias = jnp.concatenate([query_bias, blank, value_bias], axis=2)
    up_bias = up_bias.reshape(tp, 1, units)
    vectors = jnp.stack(
        [output_bias, first_gain, first_shift, down_bias, second_gain, second_shift]
    ).reshape(6, 1, width)
    output_bias, first_gain, first_shift, down_bias, second_gain, second_shift = (
        vectors[i] for i in range(6)
    )
    ids_row, ids_col = doc_ids.reshape(1, -1), doc_ids.reshape(-1, 1)

    a = Gather(jnp.concatenate([query_weight, key_weight, value_weight, output_weight.T], axis=1), steps)
    b = Gather(up_weight, steps)
    c = Gather(down_weight.T, steps)
    if direct:
        pair = Gather(jnp.stack([up_weight, down_weight.T]), steps)
        first = a.step()
        pair.held = after(pair.held, first)
        a_x = a.step(qkv_bias, up_bias, vectors, ids_row, ids_col)
        pair.step()
        a.held, pair.held = lax.optimization_barrier((a.held, pair.held))
        a.step()
        pair.step()
        a.held, pair.held = lax.optimization_barrier((a.held, pair.held))
        b, c = pair.split()
        a_x = a.step()
        b_z = b.step()
        a.pieces, b.held = lax.optimization_barrier((a.pieces, b.held))
        attn_w = ready(a.finish())
        b_x = b.step()
        c2 = c.held
        c_z = swap(after(c2, b_z), steps[2])
        c_x = swap(after(c2, b_z), steps[3])
    else:
        for package in (a, b, c):
            for _ in steps[:-1]:
                package.step()
        attn_w = ready(a.finish())
    many = len(attn_w) // 2
    parts = kept
    weight = ((parts, width, units), BF16)
    half = ((blocks_n // 2, cut_rows, units), BF16)
    side_half = ((blocks_n // 2, cut_rows + 16, units), BF16)
    state = pltpu.VMEM((SEQ, width), F32)
    turned = pltpu.VMEM((width, SEQ), BF16)
    mask = pltpu.VMEM((SEQ, SEQ), F32)
    wide, narrow = (SEQ, width), ((SEQ, width), BF16)
    full = (wide, F32)
    flipped = ((width, SEQ), BF16)
    flops = 2 * SEQ * width * width
    kept_outs = [weight, ((parts, SEQ, 3 * cols), BF16), ((parts, cols, SEQ), BF16),
                 ((parts, cols // HD, SEQ, SEQ), BF16), ((parts, 8, SEQ), F32)]
    common = (tokens, ids_row, ids_col, qkv_bias)
    *attn_first, acc, tokens_turned = call(
        partial(attention_kernel, 0), attn_w[:many], (places, turns), (*common, output_bias),
        [*kept_outs, full, flipped], [mask], 4 * flops,
    )
    *attn_second, normal, inverse, low = call(
        partial(attention_kernel, 1), attn_w[many:], (places, turns), (*common, acc, first_gain, first_shift),
        [*kept_outs, full, ((SEQ, 1), F32), narrow], [mask, state], 4 * flops,
    )
    if direct:
        up_w = b.finish(inverse, b_x)
        c_xz = swap(after(c_z, inverse, c_x), steps[3])
    else:
        up_w = ready(b.finish())
    outs = [weight, ((parts, SEQ, units), BF16), ((parts, SEQ, units), BF16)]
    up_first, active_first, slope_first, up_second, active_second, slope_second = call(
        up_kernel, up_w, (places, turns), (low, up_bias), outs * 2, [], 6 * flops
    )
    if direct:
        down_w = [after(piece, slope_second, c_xz) for piece in (c2, c_z, c_x, c_xz)]
        down_w = [c2, c_z, c_x, c_xz] + [swap(piece, steps[4]) for piece in down_w]
    else:
        down_w = ready(c.finish())
    down_first, acc = call(
        down_first_kernel, down_w[: len(down_w) // 2], (places,),
        (active_first, normal, first_gain, first_shift, down_bias), [weight, full], [], 2 * flops,
    )
    down_second, layer_output, grad_two, grad_low, grad_turned, down_sums, down_send = call(
        down_second_kernel, down_w[len(down_w) // 2 :], (places, slots),
        (active_second, acc, second_gain, second_shift, cotangent),
        [weight, full, full, narrow, flipped, ((8, width), F32), half], [state], 5 * flops,
    )
    (down_keep,) = call(
        down_third_kernel, [], (slots,), (active_first, grad_turned), [half], [], 2 * flops
    )
    down_sum = outgoing(down_keep, down_send)
    if direct:
        first = down_sum.step()
        down_sum.start()
        grad_low = after(grad_low, first)
    up_send, sums_second, acc, low_turned = call(
        partial(middle_kernel, 1), [up_second, down_second], (slots,),
        (grad_low, slope_second, grad_two, low), [half, ((8, width), F32), full, flipped], [], 6 * flops,
    )
    up_keep, sums_first, resid, resid_low, resid_turned = call(
        partial(middle_kernel, 0), [up_first, down_first], (slots,),
        (grad_low, slope_first, acc, low_turned, normal, inverse, first_gain),
        [half, ((8, width), F32), full, narrow, flipped], [state], 6 * flops,
    )
    up_sum = outgoing(up_keep, up_send)
    if direct:
        moved = down_sum.moved
        sent = down_sum.end()
        down_sum.start(sums_first)
        up_sum.start()
        up_sum.hold(resid_low, sent)
        first = up_sum.end()
        up_sum.start()
        resid_low = after(resid_low, first, sent)
    shared = jnp.concatenate([down_sums[:3], sums_first[:3]], axis=0)[None]

    def with_units(sums):
        return jnp.concatenate([jnp.broadcast_to(shared, (parts, 6, width)), sums[3 : 3 + parts, None]], axis=1)

    weight_second, *attn_second = attn_second
    weight_first, *attn_first = attn_first
    side_sums = ((parts, 8, units), F32)
    input_grad, side_second, side_first, attn_send, attn_keep = call(
        attention_back_kernel, [], (slots,),
        (tokens_turned, resid, resid_low, resid_turned, with_units(sums_second), *attn_second, weight_second,
         with_units(sums_first), *attn_first, weight_first),
        [full, side_sums, side_sums, side_half, side_half], [], 20 * flops,
    )
    attn_sum = outgoing(attn_keep, attn_send, 8)
    if direct:
        attn_sum.step(*down_sum.moved, *up_sum.moved)
        down_sum.end()
        up_sum.end()
        attn_sum.start()
        up_sum.start()
        both(attn_sum, up_sum)
        pair = Sum.merge(down_sum, up_sum)
        attn_sum.start()
        pair.start()
        both(attn_sum, pair)
        attn_sum.start()
        pair.start()
        attn_sum.end()
        finals = [[part] for part in pair.end()[0]]
        attn_sum.start()
        finals.append(attn_sum.end())
    else:
        side = jnp.concatenate([side_first, side_second], axis=0)
        finals = []
        for package in (down_sum, up_sum, attn_sum):
            while package.at > 0:
                package.step()
            package.start()
            finals.append(package.end())
    if direct:
        attn_grad, side = finals[2][0][0], finals[2][1][0]
    else:
        attn_grad = finals[2][0]
        side = lax.dynamic_index_in_dim(lax.psum(side, AXES), place, keepdims=False)
    return (
        layer_output,
        input_grad,
        attn_grad[:, :cols],
        attn_grad[:, cols : 2 * cols],
        attn_grad[:, 2 * cols : 3 * cols],
        side[7, :cols],
        side[7, 2 * cols : 3 * cols],
        attn_grad[:, 3 * cols :].T,
        side[3],
        side[4],
        side[5],
        finals[1][0],
        side[6],
        finals[0][0].T,
        side[0],
        side[1],
        side[2],
    )


def solution(mesh):
    fsdp, tp = mesh.shape["fsdp"], mesh.shape["tp"]
    steps, sources = exchange_plan(fsdp, tp)
    both, up, down = P(AXES, None), P("fsdp", "tp"), P("tp", "fsdp")
    return jax.shard_map(
        partial(shards, steps, sources, fsdp, tp),
        mesh=mesh,
        in_specs=(
            both, P("fsdp"), up, up, up, P(), P(), down, P(), P(), P(), up, P(), down, P(), P(), P(), both,
        ),
        out_specs=(
            both, both, up, up, up, P("tp"), P("tp"), down, P(), P(), P(), up, P("tp"), down, P(), P(), P(),
        ),
        check_vma=False,
    )
```

```python
from functools import partial
import math

import jax
import jax.numpy as jnp
import numpy as np
from jax import lax
from jax.experimental import pallas as pl
from jax.experimental.pallas import tpu as pltpu
from jax.sharding import PartitionSpec as P

HD = 64
SEQ = 512
AXES = ("fsdp", "tp")
F32 = jnp.float32
BF16 = jnp.bfloat16
CUTS = 8
MIB = 1 << 20


def exchange_plan(fsdp, tp):
    count = fsdp * tp
    if (fsdp, tp) == (8, 4):
        select, pairs = 1, [(8, 16), (4, 2), (16, 8), (2, 4)]
    else:
        select = tp
        pairs = [(1 << i,) * 2 for i in range(count.bit_length() - 1) if 1 << i != select]
    steps = [[d ^ pair[1 if d & select else 0] for d in range(count)] for pair in pairs]
    steps.append([d ^ select for d in range(count)])
    sources = [[d] for d in range(count)]
    for step in steps:
        sources = [sources[d] + sources[step[d]] for d in range(count)]
    return steps, np.array(sources)


def swap(array, step):
    return lax.ppermute(array, AXES, list(enumerate(step)))


def after(array, *others):
    return lax.optimization_barrier((array, *others))[0]


class Gather:
    def __init__(self, shard, steps):
        self.steps, self.at, self.held, self.pieces = steps, 0, shard[None], None

    def step(self, *others):
        step = self.steps[self.at]
        self.at += 1
        if others:
            self.held = after(self.held, *others)
        moved = swap(self.held, step)
        if self.at == len(self.steps) - 1:
            self.pieces = [self.held, moved]
        else:
            self.held = jnp.concatenate([self.held, moved], axis=0)
        return moved

    def split(self):
        parts = []
        for i in range(self.held.shape[1]):
            part = Gather(self.held[0, i], self.steps)
            part.at, part.held = self.at, self.held[:, i]
            parts.append(part)
        return parts

    def finish(self, *others):
        pieces = [after(piece, *others) for piece in self.pieces] if others else self.pieces
        return self.pieces + [swap(piece, self.steps[-1]) for piece in pieces]


class Sum:
    def __init__(self, keep, send, steps, extra=0):
        self.steps, self.at, self.keep, self.send, self.extra = steps, len(steps) - 1, keep, send, extra

    def add(self, keep, moved):
        keep, moved = keep.astype(F32), moved.astype(F32)
        if not self.extra:
            return keep + moved
        rows = keep.shape[1] - 2 * self.extra
        total = (keep + moved)[:, :rows]
        high = slice(rows, rows + self.extra)
        low = slice(rows + self.extra, None)
        side = (keep[:, high] + keep[:, low]) + (moved[:, high] + moved[:, low])
        if self.at == 0:
            return total, side
        high = lax.reduce_precision(side, 8, 7)
        return jnp.concatenate([total, high, side - high], axis=1)

    def start(self, *others):
        send = after(self.send, *others) if others else self.send
        half = send.shape[0] // 2
        parts = [send[:half], send[half:]] if self.at == len(self.steps) - 1 else [send]
        self.moved = [swap(part, self.steps[self.at]) for part in parts]

    def hold(self, *others):
        self.moved = list(lax.optimization_barrier((*self.moved, *others))[: len(self.moved)])

    def end(self):
        if self.at == 0:
            return self.add(self.keep, self.moved[0])
        half = self.keep.shape[0] // 2
        if len(self.moved) == 1:
            moved = self.moved[0][:half], self.moved[0][half:]
        else:
            moved = self.moved
        send = self.add(self.keep[half:], moved[1]).astype(BF16)
        keep = self.add(self.keep[:half], moved[0]).astype(BF16)
        self.keep, self.send = keep, send
        self.at -= 1
        return send

    def step(self, *others):
        self.start(*others)
        return self.end()

    @staticmethod
    def merge(*packages):
        one = packages[0]
        keep, send = (
            jnp.stack([getattr(package, name) for package in packages], axis=1) for name in ("keep", "send")
        )
        merged = Sum(keep, send, one.steps)
        merged.at = one.at
        return merged


def both(*packages):
    moved = lax.optimization_barrier([package.moved for package in packages])
    for package, arrived in zip(packages, moved):
        package.moved = arrived
        package.end()


def copy_block(order_ref, from_ref, to_ref):
    to_ref[...] = from_ref[...]


def laid_out(blocks, slot_of, fsdp, tp):
    _, rows, cols = blocks.shape
    grid_spec = pltpu.PrefetchScalarGridSpec(
        num_scalar_prefetch=1,
        grid=(fsdp, tp),
        in_specs=[pl.BlockSpec((1, rows, cols), lambda f, t, s: (s[f * tp + t], 0, 0))],
        out_specs=pl.BlockSpec((1, rows, cols), lambda f, t, s: (f, 0, t)),
    )
    return pl.pallas_call(
        copy_block,
        grid_spec=grid_spec,
        out_shape=jax.ShapeDtypeStruct((fsdp, rows, tp * cols), blocks.dtype),
    )(slot_of, blocks)


def cut_up(full, slot_of, fsdp, tp):
    _, rows, cols = full.shape
    cols = cols // tp
    grid_spec = pltpu.PrefetchScalarGridSpec(
        num_scalar_prefetch=1,
        grid=(fsdp, tp),
        in_specs=[pl.BlockSpec((1, rows, cols), lambda f, t, s: (f, 0, t))],
        out_specs=pl.BlockSpec((1, rows, cols), lambda f, t, s: (s[f * tp + t], 0, 0)),
    )
    return pl.pallas_call(
        copy_block,
        grid_spec=grid_spec,
        out_shape=jax.ShapeDtypeStruct((fsdp * tp, rows, cols), full.dtype),
    )(slot_of, full)


def dot(a, b):
    return lax.dot_general(a, b, (((1,), (0,)), ((), ())), preferred_element_type=F32)


def dot_nt(a, b):
    return lax.dot_general(a, b, (((1,), (1,)), ((), ())), preferred_element_type=F32)


def dot_tn(a, b):
    return lax.dot_general(a, b, (((0,), (0,)), ((), ())), preferred_element_type=F32)


def norm_forward(values):
    average = jnp.mean(values, axis=-1, keepdims=True)
    centered = values - average
    inverse = lax.rsqrt(jnp.mean(centered * centered, axis=-1, keepdims=True) + 1e-12)
    return centered * inverse, inverse


def norm_backward(upstream, normal, inverse, gain):
    scaled = upstream * gain
    return inverse * (
        scaled
        - jnp.mean(scaled, axis=-1, keepdims=True)
        - normal * jnp.mean(scaled * normal, axis=-1, keepdims=True)
    )


def gelu_parts(x):
    below = 0.5 + 0.5 * lax.erf(x * math.sqrt(0.5))
    return x * below, below + x * (jnp.exp(-0.5 * (x * x)) * (1.0 / math.sqrt(2.0 * math.pi)))


def column_sum(array):
    return jnp.sum(array, axis=0, keepdims=True)


def each(count, step):
    lax.fori_loop(0, count, lambda i, carry: (step(i), carry)[1], 0)


def assemble(half, place_ref, pieces, weight):
    rows = weight.shape[1] // CUTS
    per = pieces[0].shape[0]
    for at, piece in enumerate(pieces):

        def copy(slot, at=at, piece=piece):
            place = place_ref[(half * len(pieces) + at) * per + slot]
            i = place // CUTS
            cut = place - i * CUTS
            weight[i, pl.ds(pl.multiple_of(cut * rows, rows), rows), :] = piece[slot]

        each(per, copy)


def put_blocks(half, slot_ref, out_ref, i, value, cols=slice(None)):
    rows = value.shape[0] // CUTS
    for cut in range(CUTS):
        slot = slot_ref[half * out_ref.shape[0] + i * CUTS + cut]
        out_ref[slot, :rows, cols] = value[cut * rows : (cut + 1) * rows].astype(out_ref.dtype)


def attention_kernel(half, place_ref, turn_ref, tokens_ref, ids_row, ids_col, bias_ref, *rest):
    if half == 0:
        output_bias, *rest = rest
        *pieces, weight, qkv_ref, context_ref, exponent_ref, total_ref, acc, turned_ref, mask = rest
        acc[...] = tokens_ref[...].astype(F32) + output_bias[...]
        turned_ref[...] = tokens_ref[...].T
    else:
        acc_ref, gain, shift, *rest = rest
        *pieces, weight, qkv_ref, context_ref, exponent_ref, total_ref = rest[:-5]
        normal_ref, inverse_ref, low_ref, mask, acc = rest[-5:]
        acc[...] = acc_ref[...]
    cols = context_ref.shape[1]
    count = weight.shape[0]
    assemble(half, place_ref, pieces, weight)
    mask[...] = jnp.where(ids_col[...] == ids_row[...], 0.0, -1e30)

    def step(i):
        bias = bias_ref[turn_ref[half * count + i]]
        qkv = (dot(tokens_ref[...], weight[i, :, : 3 * cols]) + bias).astype(BF16)
        qkv_ref[i] = qkv
        contexts = []
        for h in range(cols // HD):
            queries, keys, values = (
                qkv[:, part * cols + h * HD : part * cols + (h + 1) * HD] for part in range(3)
            )
            scores = dot_nt(keys, queries * (HD**-0.5)) + mask[...]
            top = jnp.max(scores, axis=0, keepdims=True)
            exponent = jnp.exp(scores - top)
            total = 1.0 / jnp.sum(exponent, axis=0, keepdims=True)
            exponent = exponent.astype(BF16)
            exponent_ref[i, h] = exponent
            contexts.append((dot_tn(values, exponent) * total).astype(BF16))
            total_ref[i, h : h + 1] = total
        context = jnp.concatenate(contexts, axis=0)
        context_ref[i] = context
        acc[...] += dot_nt(context.T, weight[i, :, 3 * cols :])

    each(count, step)
    if half == 1:
        normal, inverse = norm_forward(acc[...])
        normal_ref[...] = normal
        inverse_ref[...] = inverse
        low_ref[...] = (normal * gain[...] + shift[...]).astype(BF16)


def up_kernel(place_ref, turn_ref, low_ref, bias_ref, *rest):
    *pieces, weight_first, active_first, slope_first, weight_second, active_second, slope_second = rest
    many = len(pieces) // 2
    up_half(0, place_ref, turn_ref, low_ref, bias_ref, pieces[:many], weight_first, active_first, slope_first)
    up_half(1, place_ref, turn_ref, low_ref, bias_ref, pieces[many:], weight_second, active_second, slope_second)


def up_half(half, place_ref, turn_ref, low_ref, bias_ref, pieces, weight, active_ref, slope_ref):
    count = weight.shape[0]
    assemble(half, place_ref, pieces, weight)

    def step(i):
        pre = dot(low_ref[...], weight[i]) + bias_ref[turn_ref[half * count + i]]
        active, slope = gelu_parts(pre)
        active_ref[i] = active.astype(BF16)
        slope_ref[i] = slope.astype(BF16)

    each(count, step)


def down_first_kernel(place_ref, active_ref, normal_ref, first_gain, first_shift, bias_ref, *rest):
    *pieces, weight, acc = rest
    assemble(0, place_ref, pieces, weight)
    acc[...] = normal_ref[...] * first_gain[...] + (first_shift[...] + bias_ref[...])

    def step(i):
        acc[...] += dot_nt(active_ref[i], weight[i])

    each(weight.shape[0], step)


def down_second_kernel(place_ref, slot_ref, active_ref, acc_ref, gain, shift, cotangent_ref, *rest):
    *pieces, weight, output_ref, grad_ref, low_ref, turned_ref, sums_ref, send_ref, acc = rest
    count = weight.shape[0]
    assemble(1, place_ref, pieces, weight)
    acc[...] = acc_ref[...]

    def step(i):
        acc[...] += dot_nt(active_ref[i], weight[i])

    each(count, step)
    normal, inverse = norm_forward(acc[...])
    output_ref[...] = normal * gain[...] + shift[...]
    upstream = cotangent_ref[...].astype(F32)
    grad = norm_backward(upstream, normal, inverse, gain[...])
    grad_ref[...] = grad
    low = grad.astype(BF16)
    low_ref[...] = low
    turned_ref[...] = low.T
    sums_ref[0:1] = column_sum(grad)
    sums_ref[1:2] = column_sum(upstream * normal)
    sums_ref[2:3] = column_sum(upstream)
    each(count, lambda i: put_blocks(1, slot_ref, send_ref, i, dot(turned_ref[...], active_ref[i])))


def down_third_kernel(slot_ref, active_ref, turned_ref, keep_ref):
    each(
        active_ref.shape[0],
        lambda i: put_blocks(0, slot_ref, keep_ref, i, dot(turned_ref[...], active_ref[i])),
    )


def middle_kernel(half, slot_ref, low_grad_ref, slope_ref, *rest):
    if half == 1:
        grad_ref, low_ref, up_w, down_w, out_ref, sums_ref, acc, turned = rest
        acc[...] = grad_ref[...]
        turned[...] = low_ref[...].T
    else:
        acc_ref, turned, normal_ref, inverse_ref, gain, up_w, down_w, *rest = rest
        out_ref, sums_ref, resid_ref, resid_low_ref, resid_turned_ref, acc = rest
        acc[...] = acc_ref[...]

    def step(i):
        wide = dot(low_grad_ref[...], down_w[i]) * slope_ref[i].astype(F32)
        pre_grad = wide.astype(BF16)
        sums_ref[pl.ds(3 + i, 1)] = column_sum(wide)
        put_blocks(half, slot_ref, out_ref, i, dot(turned[...], pre_grad))
        acc[...] += dot_nt(pre_grad, up_w[i])

    each(up_w.shape[0], step)
    if half == 0:
        grad_one = acc[...]
        normal = normal_ref[...]
        resid = norm_backward(grad_one, normal, inverse_ref[...], gain[...])
        resid_ref[...] = resid
        low = resid.astype(BF16)
        resid_low_ref[...] = low
        resid_turned_ref[...] = low.T
        sums_ref[0:1] = column_sum(resid)
        sums_ref[1:2] = column_sum(grad_one * normal)
        sums_ref[2:3] = column_sum(grad_one)


def attention_back_kernel(slot_ref, turned_ref, resid_ref, resid_low_ref, resid_turned_ref, *rest):
    *parts, grad_ref, sums_second, sums_first, send_ref, keep_ref, grads_ref = rest
    grad_ref[...] = resid_ref[...]
    many = len(parts) // 2
    shared = (slot_ref, turned_ref, resid_low_ref, resid_turned_ref, grad_ref, grads_ref)
    attention_back(1, *shared, *parts[:many], sums_second, send_ref)
    attention_back(0, *shared, *parts[many:], sums_first, keep_ref)


def attention_back(
    half, slot_ref, turned_ref, resid_low_ref, resid_turned_ref, grad_ref, grads_ref, sums_in_ref, qkv_ref, context_ref,
    exponent_ref, total_ref, weight, sums_ref, out_ref,
):
    cols = context_ref.shape[1]
    factor = HD**-0.5
    extra = sums_ref.shape[1]
    main = out_ref.shape[1] - 2 * extra

    def step(i):
        outer = dot(resid_low_ref[...], weight[i, :, 3 * cols :])
        totals = total_ref[i].T
        query_grads, key_grads, value_grads = [], [], []
        for h in range(cols // HD):
            at = slice(h * HD, (h + 1) * HD)
            queries, keys, values = (
                qkv_ref[i, :, part * cols + h * HD : part * cols + (h + 1) * HD] for part in range(3)
            )
            queries = queries * factor
            upstream = (outer[:, at] * totals[:, h : h + 1]).astype(BF16)
            row_term = jnp.sum(
                upstream.T.astype(F32) * context_ref[i, at].astype(F32), axis=0, keepdims=True
            )
            exponent = exponent_ref[i, h]
            prob_grad = dot_nt(values, upstream)
            score_grad = (exponent.astype(F32) * (prob_grad - row_term)).astype(BF16)
            key_grads.append(dot(score_grad, queries).astype(BF16))
            value_grads.append(dot(exponent, upstream).astype(BF16))
            query_grads.append((dot_tn(keys, score_grad) * factor).astype(BF16))
        queries = jnp.concatenate(query_grads, axis=0).T
        grads_ref[i] = jnp.concatenate([queries, *key_grads, *value_grads], axis=1)

    each(weight.shape[0], step)
    count = weight.shape[0]
    grad = jnp.concatenate([grads_ref[i] for i in range(count)], axis=1)
    grad_ref[...] += dot_nt(grad, jnp.concatenate([weight[i, :, : 3 * cols] for i in range(count)], axis=1))
    weight_grad = dot(turned_ref[...], grad)
    out_grad = dot_nt(resid_turned_ref[...], jnp.concatenate([context_ref[i] for i in range(count)], axis=0))
    columns = column_sum(grad.astype(F32))
    for i in range(count):
        put_blocks(half, slot_ref, out_ref, i, weight_grad[:, 3 * cols * i : 3 * cols * (i + 1)], slice(0, 3 * cols))
        put_blocks(half, slot_ref, out_ref, i, out_grad[:, cols * i : cols * (i + 1)], slice(3 * cols, None))
        side = jnp.concatenate([columns[:, 3 * cols * i : 3 * cols * (i + 1)], jnp.zeros((1, cols), F32)], axis=1)
        side = jnp.concatenate([sums_in_ref[i], side], axis=0)
        sums_ref[i] = side
        high = side.astype(BF16)
        low = (side - high.astype(F32)).astype(BF16)
        side = jnp.concatenate([high, low], axis=0)
        for cut in range(CUTS):
            out_ref[slot_ref[half * out_ref.shape[0] + i * CUTS + cut], main:, :] = side


def call(kernel, pieces, scalars, inputs, outs, scratch, flops, limit=16):
    whole = pl.BlockSpec(memory_space=pltpu.VMEM)
    smem = pl.BlockSpec(memory_space=pltpu.SMEM)
    return pl.pallas_call(
        kernel,
        in_specs=[smem] * len(scalars) + [whole] * len(inputs) + [whole] * len(pieces),
        out_specs=[whole] * len(outs),
        out_shape=[jax.ShapeDtypeStruct(*out) for out in outs],
        scratch_shapes=scratch,
        compiler_params=pltpu.CompilerParams(vmem_limit_bytes=limit * MIB),
        cost_estimate=pl.CostEstimate(flops=1024, bytes_accessed=1024, transcendentals=0),
    )(*scalars, *inputs, *pieces)


def shards(
    steps,
    sources,
    fsdp,
    tp,
    tokens,
    segment_ids,
    query_weight,
    key_weight,
    value_weight,
    query_bias,
    value_bias,
    output_weight,
    output_bias,
    first_gain,
    first_shift,
    up_weight,
    up_bias,
    down_weight,
    down_bias,
    second_gain,
    second_shift,
    cotangent,
):
    rows, cols = query_weight.shape
    width = rows * fsdp
    units = up_weight.shape[1]
    count = fsdp * tp
    cut_rows = width // CUTS
    blocks_n = CUTS * tp
    direct = blocks_n == count
    place = lax.axis_index("tp")
    me = lax.axis_index("fsdp") * tp + place
    doc_ids = lax.dynamic_slice_in_dim(segment_ids, place * SEQ, SEQ)

    def mine(table):
        return lax.dynamic_index_in_dim(jnp.asarray(table, jnp.int32), me, keepdims=False)

    slot_of = mine(np.argsort(sources, axis=1))
    kept = tp // 2
    if direct:
        sides = np.array(sources).reshape(count, 2, -1) % tp
        columns = np.sort(np.array([[np.unique(part) for part in parts] for parts in sides]), axis=2)
        inner = (sides[..., None] == columns[:, :, None, :]).argmax(axis=-1)
        spots = inner * CUTS + np.array(sources).reshape(count, 2, -1) // tp
        places = mine(spots.reshape(count, -1))
        slots = mine(np.argsort(spots, axis=2).reshape(count, -1))
        turns = mine(columns.reshape(count, -1))
    else:
        places = slots = jnp.tile(jnp.arange(blocks_n // 2, dtype=jnp.int32), 2)
        turns = jnp.arange(tp, dtype=jnp.int32)

    def ready(pieces):
        if direct:
            return pieces
        full = laid_out(jnp.concatenate(pieces, axis=0), slot_of, fsdp, tp)
        full = full.reshape(CUTS, cut_rows, tp, -1).transpose(2, 0, 1, 3)
        full = full.reshape(2, blocks_n // 2, cut_rows, -1)
        return [full[0], full[1]]

    def outgoing(keep, send, extra=0):
        if direct:
            return Sum(keep, send, steps, extra)
        blocks = jnp.concatenate([keep, send], axis=0)[:, :cut_rows]
        full = blocks.reshape(tp, CUTS, cut_rows, -1).transpose(1, 2, 0, 3)
        blocks = cut_up(full.reshape(fsdp, rows, -1), slot_of, fsdp, tp)
        return Sum(blocks[: count // 2], blocks[count // 2 :], steps)

    query_bias, value_bias = query_bias.reshape(tp, 1, cols), value_bias.reshape(tp, 1, cols)
    blank = jnp.zeros_like(query_bias)
    qkv_bias = jnp.concatenate([query_bias, blank, value_bias], axis=2)
    up_bias = up_bias.reshape(tp, 1, units)
    vectors = jnp.stack(
        [output_bias, first_gain, first_shift, down_bias, second_gain, second_shift]
    ).reshape(6, 1, width)
    output_bias, first_gain, first_shift, down_bias, second_gain, second_shift = (
        vectors[i] for i in range(6)
    )
    ids_row, ids_col = doc_ids.reshape(1, -1), doc_ids.reshape(-1, 1)

    a = Gather(jnp.concatenate([query_weight, key_weight, value_weight, output_weight.T], axis=1), steps)
    b = Gather(up_weight, steps)
    c = Gather(down_weight.T, steps)
    if direct:
        pair = Gather(jnp.stack([up_weight, down_weight.T]), steps)
        first = a.step()
        pair.held = after(pair.held, first)
        a_x = a.step(qkv_bias, up_bias, vectors, ids_row, ids_col)
        pair.step()
        a.held, pair.held = lax.optimization_barrier((a.held, pair.held))
        a.step()
        pair.step()
        a.held, pair.held = lax.optimization_barrier((a.held, pair.held))
        b, c = pair.split()
        a_x = a.step()
        b_z = b.step()
        a.pieces, b.held = lax.optimization_barrier((a.pieces, b.held))
        attn_w = ready(a.finish())
        b_x = b.step()
        c2 = c.held
        c_z = swap(after(c2, b_z), steps[2])
        c_x = swap(after(c2, b_z), steps[3])
    else:
        for package in (a, b, c):
            for _ in steps[:-1]:
                package.step()
        attn_w = ready(a.finish())
    many = len(attn_w) // 2
    parts = kept
    weight = ((parts, width, units), BF16)
    half = ((blocks_n // 2, cut_rows, units), BF16)
    side_half = ((blocks_n // 2, cut_rows + 16, units), BF16)
    state = pltpu.VMEM((SEQ, width), F32)
    turned = pltpu.VMEM((width, SEQ), BF16)
    mask = pltpu.VMEM((SEQ, SEQ), F32)
    wide, narrow = (SEQ, width), ((SEQ, width), BF16)
    full = (wide, F32)
    flipped = ((width, SEQ), BF16)
    flops = 2 * SEQ * width * width
    kept_outs = [weight, ((parts, SEQ, 3 * cols), BF16), ((parts, cols, SEQ), BF16),
                 ((parts, cols // HD, SEQ, SEQ), BF16), ((parts, 8, SEQ), F32)]
    common = (tokens, ids_row, ids_col, qkv_bias)
    *attn_first, acc, tokens_turned = call(
        partial(attention_kernel, 0), attn_w[:many], (places, turns), (*common, output_bias),
        [*kept_outs, full, flipped], [mask], 4 * flops,
    )
    *attn_second, normal, inverse, low = call(
        partial(attention_kernel, 1), attn_w[many:], (places, turns), (*common, acc, first_gain, first_shift),
        [*kept_outs, full, ((SEQ, 1), F32), narrow], [mask, state], 4 * flops,
    )
    if direct:
        up_w = b.finish(inverse, b_x)
        c_xz = swap(after(c_z, inverse, c_x), steps[3])
    else:
        up_w = ready(b.finish())
    outs = [weight, ((parts, SEQ, units), BF16), ((parts, SEQ, units), BF16)]
    up_first, active_first, slope_first, up_second, active_second, slope_second = call(
        up_kernel, up_w, (places, turns), (low, up_bias), outs * 2, [], 6 * flops
    )
    if direct:
        down_w = [after(piece, slope_second, c_xz) for piece in (c2, c_z, c_x, c_xz)]
        down_w = [c2, c_z, c_x, c_xz] + [swap(piece, steps[4]) for piece in down_w]
    else:
        down_w = ready(c.finish())
    down_first, acc = call(
        down_first_kernel, down_w[: len(down_w) // 2], (places,),
        (active_first, normal, first_gain, first_shift, down_bias), [weight, full], [], 2 * flops,
    )
    down_second, layer_output, grad_two, grad_low, grad_turned, down_sums, down_send = call(
        down_second_kernel, down_w[len(down_w) // 2 :], (places, slots),
        (active_second, acc, second_gain, second_shift, cotangent),
        [weight, full, full, narrow, flipped, ((8, width), F32), half], [state], 5 * flops,
    )
    (down_keep,) = call(
        down_third_kernel, [], (slots,), (active_first, grad_turned), [half], [], 2 * flops
    )
    down_sum = outgoing(down_keep, down_send)
    if direct:
        first = down_sum.step()
        down_sum.start()
        grad_low = after(grad_low, first)
    up_send, sums_second, acc, low_turned = call(
        partial(middle_kernel, 1), [up_second, down_second], (slots,),
        (grad_low, slope_second, grad_two, low), [half, ((8, width), F32), full, flipped], [], 6 * flops,
    )
    up_keep, sums_first, resid, resid_low, resid_turned = call(
        partial(middle_kernel, 0), [up_first, down_first], (slots,),
        (grad_low, slope_first, acc, low_turned, normal, inverse, first_gain),
        [half, ((8, width), F32), full, narrow, flipped], [state], 6 * flops,
    )
    up_sum = outgoing(up_keep, up_send)
    if direct:
        moved = down_sum.moved
        sent = down_sum.end()
        down_sum.start(sums_first)
        up_sum.start()
        up_sum.hold(resid_low, sent)
        first = up_sum.end()
        up_sum.start()
        resid_low = after(resid_low, first, sent)
    shared = jnp.concatenate([down_sums[:3], sums_first[:3]], axis=0)[None]

    def with_units(sums):
        return jnp.concatenate([jnp.broadcast_to(shared, (parts, 6, width)), sums[3 : 3 + parts, None]], axis=1)

    weight_second, *attn_second = attn_second
    weight_first, *attn_first = attn_first
    side_sums = ((parts, 8, units), F32)
    input_grad, side_second, side_first, attn_send, attn_keep = call(
        attention_back_kernel, [], (slots,),
        (tokens_turned, resid, resid_low, resid_turned, with_units(sums_second), *attn_second, weight_second,
         with_units(sums_first), *attn_first, weight_first),
        [full, side_sums, side_sums, side_half, side_half], [pltpu.VMEM((parts, SEQ, 3 * cols), BF16)], 20 * flops,
    )
    attn_sum = outgoing(attn_keep, attn_send, 8)
    if direct:
        attn_sum.step(*down_sum.moved, *up_sum.moved)
        down_sum.end()
        up_sum.end()
        attn_sum.start()
        up_sum.start()
        both(attn_sum, up_sum)
        pair = Sum.merge(down_sum, up_sum)
        attn_sum.start()
        pair.start()
        both(attn_sum, pair)
        attn_sum.start()
        pair.start()
        attn_sum.end()
        finals = [[part] for part in pair.end()[0]]
        attn_sum.start()
        finals.append(attn_sum.end())
    else:
        side = jnp.concatenate([side_first, side_second], axis=0)
        finals = []
        for package in (down_sum, up_sum, attn_sum):
            while package.at > 0:
                package.step()
            package.start()
            finals.append(package.end())
    if direct:
        attn_grad, side = finals[2][0][0], finals[2][1][0]
    else:
        attn_grad = finals[2][0]
        side = lax.dynamic_index_in_dim(lax.psum(side, AXES), place, keepdims=False)
    return (
        layer_output,
        input_grad,
        attn_grad[:, :cols],
        attn_grad[:, cols : 2 * cols],
        attn_grad[:, 2 * cols : 3 * cols],
        side[7, :cols],
        side[7, 2 * cols : 3 * cols],
        attn_grad[:, 3 * cols :].T,
        side[3],
        side[4],
        side[5],
        finals[1][0],
        side[6],
        finals[0][0].T,
        side[0],
        side[1],
        side[2],
    )


def solution(mesh):
    fsdp, tp = mesh.shape["fsdp"], mesh.shape["tp"]
    steps, sources = exchange_plan(fsdp, tp)
    both, up, down = P(AXES, None), P("fsdp", "tp"), P("tp", "fsdp")
    return jax.shard_map(
        partial(shards, steps, sources, fsdp, tp),
        mesh=mesh,
        in_specs=(
            both, P("fsdp"), up, up, up, P(), P(), down, P(), P(), P(), up, P(), down, P(), P(), P(), both,
        ),
        out_specs=(
            both, both, up, up, up, P("tp"), P("tp"), down, P(), P(), P(), up, P("tp"), down, P(), P(), P(),
        ),
        check_vma=False,
    )
```

```python
from functools import partial
import math

import jax
import jax.numpy as jnp
import numpy as np
from jax import lax
from jax.experimental import pallas as pl
from jax.experimental.pallas import tpu as pltpu
from jax.sharding import PartitionSpec as P

HD = 64
SEQ = 512
AXES = ("fsdp", "tp")
F32 = jnp.float32
BF16 = jnp.bfloat16
CUTS = 8
MIB = 1 << 20


def exchange_plan(fsdp, tp):
    count = fsdp * tp
    if (fsdp, tp) == (8, 4):
        select, pairs = 1, [(8, 16), (4, 2), (16, 8), (2, 4)]
    else:
        select = tp
        pairs = [(1 << i,) * 2 for i in range(count.bit_length() - 1) if 1 << i != select]
    steps = [[d ^ pair[1 if d & select else 0] for d in range(count)] for pair in pairs]
    steps.append([d ^ select for d in range(count)])
    sources = [[d] for d in range(count)]
    for step in steps:
        sources = [sources[d] + sources[step[d]] for d in range(count)]
    return steps, np.array(sources)


def swap(array, step):
    return lax.ppermute(array, AXES, list(enumerate(step)))


def after(array, *others):
    return lax.optimization_barrier((array, *others))[0]


class Gather:
    def __init__(self, shard, steps):
        self.steps, self.at, self.held, self.pieces = steps, 0, shard[None], None

    def step(self, *others):
        step = self.steps[self.at]
        self.at += 1
        if others:
            self.held = after(self.held, *others)
        moved = swap(self.held, step)
        if self.at == len(self.steps) - 1:
            self.pieces = [self.held, moved]
        else:
            self.held = jnp.concatenate([self.held, moved], axis=0)
        return moved

    def split(self):
        parts = []
        for i in range(self.held.shape[1]):
            part = Gather(self.held[0, i], self.steps)
            part.at, part.held = self.at, self.held[:, i]
            parts.append(part)
        return parts

    def finish(self, *others):
        pieces = [after(piece, *others) for piece in self.pieces] if others else self.pieces
        return self.pieces + [swap(piece, self.steps[-1]) for piece in pieces]


class Sum:
    def __init__(self, keep, send, steps, extra=0):
        self.steps, self.at, self.keep, self.send, self.extra = steps, len(steps) - 1, keep, send, extra

    def add(self, keep, moved):
        keep, moved = keep.astype(F32), moved.astype(F32)
        if not self.extra:
            return keep + moved
        rows = keep.shape[1] - 2 * self.extra
        total = (keep + moved)[:, :rows]
        high = slice(rows, rows + self.extra)
        low = slice(rows + self.extra, None)
        side = (keep[:, high] + keep[:, low]) + (moved[:, high] + moved[:, low])
        if self.at == 0:
            return total, side
        high = lax.reduce_precision(side, 8, 7)
        return jnp.concatenate([total, high, side - high], axis=1)

    def start(self, *others):
        send = after(self.send, *others) if others else self.send
        half = send.shape[0] // 2
        parts = [send[:half], send[half:]] if self.at == len(self.steps) - 1 else [send]
        self.moved = [swap(part, self.steps[self.at]) for part in parts]

    def hold(self, *others):
        self.moved = list(lax.optimization_barrier((*self.moved, *others))[: len(self.moved)])

    def end(self):
        if self.at == 0:
            return self.add(self.keep, self.moved[0])
        half = self.keep.shape[0] // 2
        if len(self.moved) == 1:
            moved = self.moved[0][:half], self.moved[0][half:]
        else:
            moved = self.moved
        send = self.add(self.keep[half:], moved[1]).astype(BF16)
        keep = self.add(self.keep[:half], moved[0]).astype(BF16)
        self.keep, self.send = keep, send
        self.at -= 1
        return send

    def step(self, *others):
        self.start(*others)
        return self.end()

    @staticmethod
    def merge(*packages):
        one = packages[0]
        keep, send = (
            jnp.stack([getattr(package, name) for package in packages], axis=1) for name in ("keep", "send")
        )
        merged = Sum(keep, send, one.steps)
        merged.at = one.at
        return merged


def both(*packages):
    moved = lax.optimization_barrier([package.moved for package in packages])
    for package, arrived in zip(packages, moved):
        package.moved = arrived
        package.end()


def copy_block(order_ref, from_ref, to_ref):
    to_ref[...] = from_ref[...]


def laid_out(blocks, slot_of, fsdp, tp):
    _, rows, cols = blocks.shape
    grid_spec = pltpu.PrefetchScalarGridSpec(
        num_scalar_prefetch=1,
        grid=(fsdp, tp),
        in_specs=[pl.BlockSpec((1, rows, cols), lambda f, t, s: (s[f * tp + t], 0, 0))],
        out_specs=pl.BlockSpec((1, rows, cols), lambda f, t, s: (f, 0, t)),
    )
    return pl.pallas_call(
        copy_block,
        grid_spec=grid_spec,
        out_shape=jax.ShapeDtypeStruct((fsdp, rows, tp * cols), blocks.dtype),
    )(slot_of, blocks)


def cut_up(full, slot_of, fsdp, tp):
    _, rows, cols = full.shape
    cols = cols // tp
    grid_spec = pltpu.PrefetchScalarGridSpec(
        num_scalar_prefetch=1,
        grid=(fsdp, tp),
        in_specs=[pl.BlockSpec((1, rows, cols), lambda f, t, s: (f, 0, t))],
        out_specs=pl.BlockSpec((1, rows, cols), lambda f, t, s: (s[f * tp + t], 0, 0)),
    )
    return pl.pallas_call(
        copy_block,
        grid_spec=grid_spec,
        out_shape=jax.ShapeDtypeStruct((fsdp * tp, rows, cols), full.dtype),
    )(slot_of, full)


def dot(a, b):
    return lax.dot_general(a, b, (((1,), (0,)), ((), ())), preferred_element_type=F32)


def dot_nt(a, b):
    return lax.dot_general(a, b, (((1,), (1,)), ((), ())), preferred_element_type=F32)


def dot_tn(a, b):
    return lax.dot_general(a, b, (((0,), (0,)), ((), ())), preferred_element_type=F32)


def norm_forward(values):
    average = jnp.mean(values, axis=-1, keepdims=True)
    centered = values - average
    inverse = lax.rsqrt(jnp.mean(centered * centered, axis=-1, keepdims=True) + 1e-12)
    return centered * inverse, inverse


def norm_backward(upstream, normal, inverse, gain):
    scaled = upstream * gain
    return inverse * (
        scaled
        - jnp.mean(scaled, axis=-1, keepdims=True)
        - normal * jnp.mean(scaled * normal, axis=-1, keepdims=True)
    )


def gelu_parts(x):
    below = 0.5 + 0.5 * lax.erf(x * math.sqrt(0.5))
    return x * below, below + x * (jnp.exp(-0.5 * (x * x)) * (1.0 / math.sqrt(2.0 * math.pi)))


def column_sum(array):
    return jnp.sum(array, axis=0, keepdims=True)


def each(count, step):
    lax.fori_loop(0, count, lambda i, carry: (step(i), carry)[1], 0)


def assemble(half, place_ref, pieces, weight):
    rows = weight.shape[1] // CUTS
    per = pieces[0].shape[0]
    for at, piece in enumerate(pieces):

        def copy(slot, at=at, piece=piece):
            place = place_ref[(half * len(pieces) + at) * per + slot]
            i = place // CUTS
            cut = place - i * CUTS
            weight[i, pl.ds(pl.multiple_of(cut * rows, rows), rows), :] = piece[slot]

        each(per, copy)


def put_blocks(half, slot_ref, out_ref, i, value, cols=slice(None)):
    rows = value.shape[0] // CUTS
    for cut in range(CUTS):
        slot = slot_ref[half * out_ref.shape[0] + i * CUTS + cut]
        out_ref[slot, :rows, cols] = value[cut * rows : (cut + 1) * rows].astype(out_ref.dtype)


def attention_kernel(half, place_ref, turn_ref, tokens_ref, ids_row, ids_col, bias_ref, *rest):
    if half == 0:
        output_bias, *rest = rest
        *pieces, weight, qkv_ref, context_ref, exponent_ref, total_ref, acc, turned_ref, mask = rest
        acc[...] = tokens_ref[...].astype(F32) + output_bias[...]
        turned_ref[...] = tokens_ref[...].T
    else:
        acc_ref, gain, shift, *rest = rest
        *pieces, weight, qkv_ref, context_ref, exponent_ref, total_ref = rest[:-5]
        normal_ref, inverse_ref, low_ref, mask, acc = rest[-5:]
        acc[...] = acc_ref[...]
    cols = context_ref.shape[1]
    count = weight.shape[0]
    assemble(half, place_ref, pieces, weight)
    mask[...] = jnp.where(ids_col[...] == ids_row[...], 0.0, -1e30)

    def step(i):
        bias = bias_ref[turn_ref[half * count + i]]
        qkv = (dot(tokens_ref[...], weight[i, :, : 3 * cols]) + bias).astype(BF16)
        qkv_ref[i] = qkv
        contexts = []
        for h in range(cols // HD):
            queries, keys, values = (
                qkv[:, part * cols + h * HD : part * cols + (h + 1) * HD] for part in range(3)
            )
            scores = dot_nt(keys, queries * (HD**-0.5)) + mask[...]
            top = jnp.max(scores, axis=0, keepdims=True)
            exponent = jnp.exp(scores - top)
            total = 1.0 / jnp.sum(exponent, axis=0, keepdims=True)
            exponent = exponent.astype(BF16)
            exponent_ref[i, h] = exponent
            contexts.append((dot_tn(values, exponent) * total).astype(BF16))
            total_ref[i, h : h + 1] = total
        context = jnp.concatenate(contexts, axis=0)
        context_ref[i] = context
        acc[...] += dot_nt(context.T, weight[i, :, 3 * cols :])

    each(count, step)
    if half == 1:
        normal, inverse = norm_forward(acc[...])
        normal_ref[...] = normal
        inverse_ref[...] = inverse
        low_ref[...] = (normal * gain[...] + shift[...]).astype(BF16)


def up_kernel(place_ref, turn_ref, low_ref, bias_ref, *rest):
    *pieces, weight_first, active_first, slope_first, weight_second, active_second, slope_second = rest
    many = len(pieces) // 2
    up_half(0, place_ref, turn_ref, low_ref, bias_ref, pieces[:many], weight_first, active_first, slope_first)
    up_half(1, place_ref, turn_ref, low_ref, bias_ref, pieces[many:], weight_second, active_second, slope_second)


def up_half(half, place_ref, turn_ref, low_ref, bias_ref, pieces, weight, active_ref, slope_ref):
    count = weight.shape[0]
    assemble(half, place_ref, pieces, weight)

    def step(i):
        pre = dot(low_ref[...], weight[i]) + bias_ref[turn_ref[half * count + i]]
        active, slope = gelu_parts(pre)
        active_ref[i] = active.astype(BF16)
        slope_ref[i] = slope.astype(BF16)

    each(count, step)


def down_first_kernel(place_ref, active_ref, normal_ref, first_gain, first_shift, bias_ref, *rest):
    *pieces, weight, acc = rest
    assemble(0, place_ref, pieces, weight)
    acc[...] = normal_ref[...] * first_gain[...] + (first_shift[...] + bias_ref[...])

    def step(i):
        acc[...] += dot_nt(active_ref[i], weight[i])

    each(weight.shape[0], step)


def down_second_kernel(place_ref, slot_ref, active_ref, acc_ref, gain, shift, cotangent_ref, *rest):
    *pieces, weight, output_ref, grad_ref, low_ref, turned_ref, sums_ref, send_ref, acc = rest
    count = weight.shape[0]
    assemble(1, place_ref, pieces, weight)
    acc[...] = acc_ref[...]

    def step(i):
        acc[...] += dot_nt(active_ref[i], weight[i])

    each(count, step)
    normal, inverse = norm_forward(acc[...])
    output_ref[...] = normal * gain[...] + shift[...]
    upstream = cotangent_ref[...].astype(F32)
    grad = norm_backward(upstream, normal, inverse, gain[...])
    grad_ref[...] = grad
    low = grad.astype(BF16)
    low_ref[...] = low
    turned_ref[...] = low.T
    sums_ref[0:1] = column_sum(grad)
    sums_ref[1:2] = column_sum(upstream * normal)
    sums_ref[2:3] = column_sum(upstream)
    each(count, lambda i: put_blocks(1, slot_ref, send_ref, i, dot(turned_ref[...], active_ref[i])))


def down_third_kernel(slot_ref, active_ref, turned_ref, keep_ref):
    each(
        active_ref.shape[0],
        lambda i: put_blocks(0, slot_ref, keep_ref, i, dot(turned_ref[...], active_ref[i])),
    )


def middle_kernel(half, slot_ref, low_grad_ref, slope_ref, *rest):
    if half == 1:
        grad_ref, low_ref, up_w, down_w, out_ref, sums_ref, acc, turned = rest
        acc[...] = grad_ref[...]
        turned[...] = low_ref[...].T
    else:
        acc_ref, turned, normal_ref, inverse_ref, gain, up_w, down_w, *rest = rest
        out_ref, sums_ref, resid_ref, resid_low_ref, resid_turned_ref, acc = rest
        acc[...] = acc_ref[...]

    def step(i):
        wide = dot(low_grad_ref[...], down_w[i]) * slope_ref[i].astype(F32)
        pre_grad = wide.astype(BF16)
        sums_ref[pl.ds(3 + i, 1)] = column_sum(wide)
        put_blocks(half, slot_ref, out_ref, i, dot(turned[...], pre_grad))
        acc[...] += dot_nt(pre_grad, up_w[i])

    each(up_w.shape[0], step)
    if half == 0:
        grad_one = acc[...]
        normal = normal_ref[...]
        resid = norm_backward(grad_one, normal, inverse_ref[...], gain[...])
        resid_ref[...] = resid
        low = resid.astype(BF16)
        resid_low_ref[...] = low
        resid_turned_ref[...] = low.T
        sums_ref[0:1] = column_sum(resid)
        sums_ref[1:2] = column_sum(grad_one * normal)
        sums_ref[2:3] = column_sum(grad_one)


def attention_back_kernel(slot_ref, turned_ref, resid_ref, resid_low_ref, resid_turned_ref, *rest):
    *parts, grad_ref, sums_second, sums_first, send_ref, keep_ref, grads_ref = rest
    grad_ref[...] = resid_ref[...]
    many = len(parts) // 2
    shared = (slot_ref, turned_ref, resid_low_ref, resid_turned_ref, grad_ref, grads_ref)
    attention_back(1, *shared, *parts[:many], sums_second, send_ref)
    attention_back(0, *shared, *parts[many:], sums_first, keep_ref)


def attention_back(
    half, slot_ref, turned_ref, resid_low_ref, resid_turned_ref, grad_ref, grads_ref, sums_in_ref, qkv_ref, context_ref,
    exponent_ref, total_ref, weight, sums_ref, out_ref,
):
    cols = context_ref.shape[1]
    factor = HD**-0.5
    extra = sums_ref.shape[1]
    main = out_ref.shape[1] - 2 * extra

    def step(i):
        outer = dot(resid_low_ref[...], weight[i, :, 3 * cols :])
        totals = total_ref[i].T
        query_grads, key_grads, value_grads = [], [], []
        for h in range(cols // HD):
            at = slice(h * HD, (h + 1) * HD)
            queries, keys, values = (
                qkv_ref[i, :, part * cols + h * HD : part * cols + (h + 1) * HD] for part in range(3)
            )
            queries = queries * factor
            upstream = (outer[:, at] * totals[:, h : h + 1]).astype(BF16)
            row_term = jnp.sum(
                upstream.T.astype(F32) * context_ref[i, at].astype(F32), axis=0, keepdims=True
            )
            exponent = exponent_ref[i, h]
            prob_grad = dot_nt(values, upstream)
            score_grad = (exponent.astype(F32) * (prob_grad - row_term)).astype(BF16)
            key_grads.append(dot(score_grad, queries).astype(BF16))
            value_grads.append(dot(exponent, upstream).astype(BF16))
            query_grads.append((dot_tn(keys, score_grad) * factor).astype(BF16))
        queries = jnp.concatenate(query_grads, axis=0).T
        grads_ref[i] = jnp.concatenate([queries, *key_grads, *value_grads], axis=1)

    each(weight.shape[0], step)
    count = weight.shape[0]
    grad = jnp.concatenate([grads_ref[i] for i in range(count)], axis=1)
    grad_ref[...] += dot_nt(grad, jnp.concatenate([weight[i, :, : 3 * cols] for i in range(count)], axis=1))
    weight_grad = dot(turned_ref[...], grad)
    out_grad = dot_nt(resid_turned_ref[...], jnp.concatenate([context_ref[i] for i in range(count)], axis=0))
    columns = column_sum(grad.astype(F32))
    for i in range(count):
        put_blocks(half, slot_ref, out_ref, i, weight_grad[:, 3 * cols * i : 3 * cols * (i + 1)], slice(0, 3 * cols))
        put_blocks(half, slot_ref, out_ref, i, out_grad[:, cols * i : cols * (i + 1)], slice(3 * cols, None))
        side = jnp.concatenate([columns[:, 3 * cols * i : 3 * cols * (i + 1)], jnp.zeros((1, cols), F32)], axis=1)
        side = jnp.concatenate([sums_in_ref[i], side], axis=0)
        sums_ref[i] = side
        high = side.astype(BF16)
        low = (side - high.astype(F32)).astype(BF16)
        side = jnp.concatenate([high, low], axis=0)
        for cut in range(CUTS):
            out_ref[slot_ref[half * out_ref.shape[0] + i * CUTS + cut], main:, :] = side


def unpack_kernel(keep_ref, moved_ref, query_ref, key_ref, value_ref, out_ref, side_ref):
    total = keep_ref[0].astype(F32) + moved_ref[0].astype(F32)
    rows, cols = query_ref.shape
    extra = side_ref.shape[0]
    for i, ref in enumerate((query_ref, key_ref, value_ref)):
        ref[...] = total[:rows, i * cols : (i + 1) * cols]
    out_ref[...] = total[:rows, 3 * cols :].T
    side_ref[...] = total[rows : rows + extra] + total[rows + extra :]


def call(kernel, pieces, scalars, inputs, outs, scratch, flops, limit=16):
    whole = pl.BlockSpec(memory_space=pltpu.VMEM)
    smem = pl.BlockSpec(memory_space=pltpu.SMEM)
    return pl.pallas_call(
        kernel,
        in_specs=[smem] * len(scalars) + [whole] * len(inputs) + [whole] * len(pieces),
        out_specs=[whole] * len(outs),
        out_shape=[jax.ShapeDtypeStruct(*out) for out in outs],
        scratch_shapes=scratch,
        compiler_params=pltpu.CompilerParams(vmem_limit_bytes=limit * MIB),
        cost_estimate=pl.CostEstimate(flops=1024, bytes_accessed=1024, transcendentals=0),
    )(*scalars, *inputs, *pieces)


def shards(
    steps,
    sources,
    fsdp,
    tp,
    tokens,
    segment_ids,
    query_weight,
    key_weight,
    value_weight,
    query_bias,
    value_bias,
    output_weight,
    output_bias,
    first_gain,
    first_shift,
    up_weight,
    up_bias,
    down_weight,
    down_bias,
    second_gain,
    second_shift,
    cotangent,
):
    rows, cols = query_weight.shape
    width = rows * fsdp
    units = up_weight.shape[1]
    count = fsdp * tp
    cut_rows = width // CUTS
    blocks_n = CUTS * tp
    direct = blocks_n == count
    place = lax.axis_index("tp")
    me = lax.axis_index("fsdp") * tp + place
    doc_ids = lax.dynamic_slice_in_dim(segment_ids, place * SEQ, SEQ)

    def mine(table):
        return lax.dynamic_index_in_dim(jnp.asarray(table, jnp.int32), me, keepdims=False)

    slot_of = mine(np.argsort(sources, axis=1))
    kept = tp // 2
    if direct:
        sides = np.array(sources).reshape(count, 2, -1) % tp
        columns = np.sort(np.array([[np.unique(part) for part in parts] for parts in sides]), axis=2)
        inner = (sides[..., None] == columns[:, :, None, :]).argmax(axis=-1)
        spots = inner * CUTS + np.array(sources).reshape(count, 2, -1) // tp
        places = mine(spots.reshape(count, -1))
        slots = mine(np.argsort(spots, axis=2).reshape(count, -1))
        turns = mine(columns.reshape(count, -1))
    else:
        places = slots = jnp.tile(jnp.arange(blocks_n // 2, dtype=jnp.int32), 2)
        turns = jnp.arange(tp, dtype=jnp.int32)

    def ready(pieces):
        if direct:
            return pieces
        full = laid_out(jnp.concatenate(pieces, axis=0), slot_of, fsdp, tp)
        full = full.reshape(CUTS, cut_rows, tp, -1).transpose(2, 0, 1, 3)
        full = full.reshape(2, blocks_n // 2, cut_rows, -1)
        return [full[0], full[1]]

    def outgoing(keep, send, extra=0):
        if direct:
            return Sum(keep, send, steps, extra)
        blocks = jnp.concatenate([keep, send], axis=0)[:, :cut_rows]
        full = blocks.reshape(tp, CUTS, cut_rows, -1).transpose(1, 2, 0, 3)
        blocks = cut_up(full.reshape(fsdp, rows, -1), slot_of, fsdp, tp)
        return Sum(blocks[: count // 2], blocks[count // 2 :], steps)

    query_bias, value_bias = query_bias.reshape(tp, 1, cols), value_bias.reshape(tp, 1, cols)
    blank = jnp.zeros_like(query_bias)
    qkv_bias = jnp.concatenate([query_bias, blank, value_bias], axis=2)
    up_bias = up_bias.reshape(tp, 1, units)
    vectors = jnp.stack(
        [output_bias, first_gain, first_shift, down_bias, second_gain, second_shift]
    ).reshape(6, 1, width)
    output_bias, first_gain, first_shift, down_bias, second_gain, second_shift = (
        vectors[i] for i in range(6)
    )
    ids_row, ids_col = doc_ids.reshape(1, -1), doc_ids.reshape(-1, 1)

    a = Gather(jnp.concatenate([query_weight, key_weight, value_weight, output_weight.T], axis=1), steps)
    b = Gather(up_weight, steps)
    c = Gather(down_weight.T, steps)
    if direct:
        pair = Gather(jnp.stack([up_weight, down_weight.T]), steps)
        first = a.step()
        pair.held = after(pair.held, first)
        a_x = a.step(qkv_bias, up_bias, vectors, ids_row, ids_col)
        pair.step()
        a.held, pair.held = lax.optimization_barrier((a.held, pair.held))
        a.step()
        pair.step()
        a.held, pair.held = lax.optimization_barrier((a.held, pair.held))
        b, c = pair.split()
        a_x = a.step()
        b_z = b.step()
        a.pieces, b.held = lax.optimization_barrier((a.pieces, b.held))
        attn_w = ready(a.finish())
        b_x = b.step()
        c2 = c.held
        c_z = swap(after(c2, b_z), steps[2])
        c_x = swap(after(c2, b_z), steps[3])
    else:
        for package in (a, b, c):
            for _ in steps[:-1]:
                package.step()
        attn_w = ready(a.finish())
    many = len(attn_w) // 2
    parts = kept
    weight = ((parts, width, units), BF16)
    half = ((blocks_n // 2, cut_rows, units), BF16)
    side_half = ((blocks_n // 2, cut_rows + 16, units), BF16)
    state = pltpu.VMEM((SEQ, width), F32)
    turned = pltpu.VMEM((width, SEQ), BF16)
    mask = pltpu.VMEM((SEQ, SEQ), F32)
    wide, narrow = (SEQ, width), ((SEQ, width), BF16)
    full = (wide, F32)
    flipped = ((width, SEQ), BF16)
    flops = 2 * SEQ * width * width
    kept_outs = [weight, ((parts, SEQ, 3 * cols), BF16), ((parts, cols, SEQ), BF16),
                 ((parts, cols // HD, SEQ, SEQ), BF16), ((parts, 8, SEQ), F32)]
    common = (tokens, ids_row, ids_col, qkv_bias)
    *attn_first, acc, tokens_turned = call(
        partial(attention_kernel, 0), attn_w[:many], (places, turns), (*common, output_bias),
        [*kept_outs, full, flipped], [mask], 4 * flops,
    )
    *attn_second, normal, inverse, low = call(
        partial(attention_kernel, 1), attn_w[many:], (places, turns), (*common, acc, first_gain, first_shift),
        [*kept_outs, full, ((SEQ, 1), F32), narrow], [mask, state], 4 * flops,
    )
    if direct:
        up_w = b.finish(inverse, b_x)
        c_xz = swap(after(c_z, inverse, c_x), steps[3])
    else:
        up_w = ready(b.finish())
    outs = [weight, ((parts, SEQ, units), BF16), ((parts, SEQ, units), BF16)]
    up_first, active_first, slope_first, up_second, active_second, slope_second = call(
        up_kernel, up_w, (places, turns), (low, up_bias), outs * 2, [], 6 * flops
    )
    if direct:
        down_w = [after(piece, slope_second, c_xz) for piece in (c2, c_z, c_x, c_xz)]
        down_w = [c2, c_z, c_x, c_xz] + [swap(piece, steps[4]) for piece in down_w]
    else:
        down_w = ready(c.finish())
    down_first, acc = call(
        down_first_kernel, down_w[: len(down_w) // 2], (places,),
        (active_first, normal, first_gain, first_shift, down_bias), [weight, full], [], 2 * flops,
    )
    down_second, layer_output, grad_two, grad_low, grad_turned, down_sums, down_send = call(
        down_second_kernel, down_w[len(down_w) // 2 :], (places, slots),
        (active_second, acc, second_gain, second_shift, cotangent),
        [weight, full, full, narrow, flipped, ((8, width), F32), half], [state], 5 * flops,
    )
    (down_keep,) = call(
        down_third_kernel, [], (slots,), (active_first, grad_turned), [half], [], 2 * flops
    )
    down_sum = outgoing(down_keep, down_send)
    if direct:
        first = down_sum.step()
        down_sum.start()
        grad_low = after(grad_low, first)
    up_send, sums_second, acc, low_turned = call(
        partial(middle_kernel, 1), [up_second, down_second], (slots,),
        (grad_low, slope_second, grad_two, low), [half, ((8, width), F32), full, flipped], [], 6 * flops,
    )
    up_keep, sums_first, resid, resid_low, resid_turned = call(
        partial(middle_kernel, 0), [up_first, down_first], (slots,),
        (grad_low, slope_first, acc, low_turned, normal, inverse, first_gain),
        [half, ((8, width), F32), full, narrow, flipped], [state], 6 * flops,
    )
    up_sum = outgoing(up_keep, up_send)
    if direct:
        moved = down_sum.moved
        sent = down_sum.end()
        down_sum.start(sums_first)
        up_sum.start()
        up_sum.hold(resid_low, sent)
        first = up_sum.end()
        up_sum.start()
        resid_low = after(resid_low, first, sent)
    shared = jnp.concatenate([down_sums[:3], sums_first[:3]], axis=0)[None]

    def with_units(sums):
        return jnp.concatenate([jnp.broadcast_to(shared, (parts, 6, width)), sums[3 : 3 + parts, None]], axis=1)

    weight_second, *attn_second = attn_second
    weight_first, *attn_first = attn_first
    side_sums = ((parts, 8, units), F32)
    input_grad, side_second, side_first, attn_send, attn_keep = call(
        attention_back_kernel, [], (slots,),
        (tokens_turned, resid, resid_low, resid_turned, with_units(sums_second), *attn_second, weight_second,
         with_units(sums_first), *attn_first, weight_first),
        [full, side_sums, side_sums, side_half, side_half], [pltpu.VMEM((parts, SEQ, 3 * cols), BF16)], 20 * flops,
    )
    attn_sum = outgoing(attn_keep, attn_send, 8)
    if direct:
        attn_sum.start(*down_sum.moved, *up_sum.moved)
        down_sum.end()
        up_sum.end()
        keep, moved = attn_sum.keep, attn_sum.moved
        part = keep.shape[0] // 4
        last = swap(attn_sum.add(keep[3 * part :], moved[1][part:]).astype(BF16), steps[3])
        up_sum.start()
        third = attn_sum.add(keep[2 * part : 3 * part], moved[1][:part]).astype(BF16)
        third = swap(after(third, last), steps[3])
        second = attn_sum.add(keep[part : 2 * part], moved[0][part:]).astype(BF16)
        attn_sum.moved = [swap(attn_sum.add(second, last).astype(BF16), steps[2])]
        first = attn_sum.add(keep[:part], moved[0][:part]).astype(BF16)
        attn_sum.keep, attn_sum.at = attn_sum.add(first, third).astype(BF16), 2
        up_sum.hold(last)
        up_sum.end()
        pair = Sum.merge(down_sum, up_sum)
        pair.start(third)
        both(attn_sum, pair)
        attn_sum.start()
        pair.start()
        attn_sum.end()
        finals = [[part] for part in pair.end()[0]]
        attn_sum.start()
    else:
        side = jnp.concatenate([side_first, side_second], axis=0)
        finals = []
        for package in (down_sum, up_sum, attn_sum):
            while package.at > 0:
                package.step()
            package.start()
            finals.append(package.end())
    if direct:
        small = ((rows, cols), F32)
        query_grad, key_grad, value_grad, out_grad, side = call(
            unpack_kernel, [], (), (attn_sum.keep, *attn_sum.moved),
            [small, small, small, ((cols, rows), F32), ((8, width), F32)], [], 1,
        )
    else:
        attn_grad = finals[2][0]
        query_grad, key_grad, value_grad = (attn_grad[:, i * cols : (i + 1) * cols] for i in range(3))
        out_grad = attn_grad[:, 3 * cols :].T
        side = lax.dynamic_index_in_dim(lax.psum(side, AXES), place, keepdims=False)
    return (
        layer_output,
        input_grad,
        query_grad,
        key_grad,
        value_grad,
        side[7, :cols],
        side[7, 2 * cols : 3 * cols],
        out_grad,
        side[3],
        side[4],
        side[5],
        finals[1][0],
        side[6],
        finals[0][0].T,
        side[0],
        side[1],
        side[2],
    )


def solution(mesh):
    fsdp, tp = mesh.shape["fsdp"], mesh.shape["tp"]
    steps, sources = exchange_plan(fsdp, tp)
    both, up, down = P(AXES, None), P("fsdp", "tp"), P("tp", "fsdp")
    return jax.shard_map(
        partial(shards, steps, sources, fsdp, tp),
        mesh=mesh,
        in_specs=(
            both, P("fsdp"), up, up, up, P(), P(), down, P(), P(), P(), up, P(), down, P(), P(), P(), both,
        ),
        out_specs=(
            both, both, up, up, up, P("tp"), P("tp"), down, P(), P(), P(), up, P("tp"), down, P(), P(), P(),
        ),
        check_vma=False,
    )
```

```python
from functools import partial
import math

import jax
import jax.numpy as jnp
import numpy as np
from jax import lax
from jax.experimental import pallas as pl
from jax.experimental.pallas import tpu as pltpu
from jax.sharding import PartitionSpec as P

HD = 64
SEQ = 512
AXES = ("fsdp", "tp")
F32 = jnp.float32
BF16 = jnp.bfloat16
CUTS = 8
MIB = 1 << 20


def exchange_plan(fsdp, tp):
    count = fsdp * tp
    if (fsdp, tp) == (8, 4):
        select, pairs = 1, [(8, 16), (4, 2), (16, 8), (2, 4)]
    else:
        select = tp
        pairs = [(1 << i,) * 2 for i in range(count.bit_length() - 1) if 1 << i != select]
    steps = [[d ^ pair[1 if d & select else 0] for d in range(count)] for pair in pairs]
    steps.append([d ^ select for d in range(count)])
    sources = [[d] for d in range(count)]
    for step in steps:
        sources = [sources[d] + sources[step[d]] for d in range(count)]
    return steps, np.array(sources)


def swap(array, step):
    return lax.ppermute(array, AXES, list(enumerate(step)))


def after(array, *others):
    return lax.optimization_barrier((array, *others))[0]


class Gather:
    def __init__(self, shard, steps):
        self.steps, self.at, self.held, self.pieces = steps, 0, shard[None], None

    def step(self, *others):
        step = self.steps[self.at]
        self.at += 1
        if others:
            self.held = after(self.held, *others)
        moved = swap(self.held, step)
        if self.at == len(self.steps) - 1:
            self.pieces = [self.held, moved]
        else:
            self.held = jnp.concatenate([self.held, moved], axis=0)
        return moved

    def split(self):
        parts = []
        for i in range(self.held.shape[1]):
            part = Gather(self.held[0, i], self.steps)
            part.at, part.held = self.at, self.held[:, i]
            parts.append(part)
        return parts

    def finish(self, *others):
        pieces = [after(piece, *others) for piece in self.pieces] if others else self.pieces
        return self.pieces + [swap(piece, self.steps[-1]) for piece in pieces]


class Sum:
    def __init__(self, keep, send, steps, extra=0):
        self.steps, self.at, self.keep, self.send, self.extra = steps, len(steps) - 1, keep, send, extra

    def add(self, keep, moved):
        keep, moved = keep.astype(F32), moved.astype(F32)
        if not self.extra:
            return keep + moved
        rows = keep.shape[1] - 2 * self.extra
        total = (keep + moved)[:, :rows]
        high = slice(rows, rows + self.extra)
        low = slice(rows + self.extra, None)
        side = (keep[:, high] + keep[:, low]) + (moved[:, high] + moved[:, low])
        if self.at == 0:
            return total, side
        high = lax.reduce_precision(side, 8, 7)
        return jnp.concatenate([total, high, side - high], axis=1)

    def start(self, *others):
        send = after(self.send, *others) if others else self.send
        half = send.shape[0] // 2
        parts = [send[:half], send[half:]] if self.at == len(self.steps) - 1 else [send]
        self.moved = [swap(part, self.steps[self.at]) for part in parts]

    def hold(self, *others):
        self.moved = list(lax.optimization_barrier((*self.moved, *others))[: len(self.moved)])

    def end(self):
        if self.at == 0:
            return self.add(self.keep, self.moved[0])
        half = self.keep.shape[0] // 2
        if len(self.moved) == 1:
            moved = self.moved[0][:half], self.moved[0][half:]
        else:
            moved = self.moved
        send = self.add(self.keep[half:], moved[1]).astype(BF16)
        keep = self.add(self.keep[:half], moved[0]).astype(BF16)
        self.keep, self.send = keep, send
        self.at -= 1
        return send

    def step(self, *others):
        self.start(*others)
        return self.end()

    @staticmethod
    def merge(*packages):
        one = packages[0]
        keep, send = (
            jnp.stack([getattr(package, name) for package in packages], axis=1) for name in ("keep", "send")
        )
        merged = Sum(keep, send, one.steps)
        merged.at = one.at
        return merged


def both(*packages):
    moved = lax.optimization_barrier([package.moved for package in packages])
    for package, arrived in zip(packages, moved):
        package.moved = arrived
        package.end()


def copy_block(order_ref, from_ref, to_ref):
    to_ref[...] = from_ref[...]


def laid_out(blocks, slot_of, fsdp, tp):
    _, rows, cols = blocks.shape
    grid_spec = pltpu.PrefetchScalarGridSpec(
        num_scalar_prefetch=1,
        grid=(fsdp, tp),
        in_specs=[pl.BlockSpec((1, rows, cols), lambda f, t, s: (s[f * tp + t], 0, 0))],
        out_specs=pl.BlockSpec((1, rows, cols), lambda f, t, s: (f, 0, t)),
    )
    return pl.pallas_call(
        copy_block,
        grid_spec=grid_spec,
        out_shape=jax.ShapeDtypeStruct((fsdp, rows, tp * cols), blocks.dtype),
    )(slot_of, blocks)


def cut_up(full, slot_of, fsdp, tp):
    _, rows, cols = full.shape
    cols = cols // tp
    grid_spec = pltpu.PrefetchScalarGridSpec(
        num_scalar_prefetch=1,
        grid=(fsdp, tp),
        in_specs=[pl.BlockSpec((1, rows, cols), lambda f, t, s: (f, 0, t))],
        out_specs=pl.BlockSpec((1, rows, cols), lambda f, t, s: (s[f * tp + t], 0, 0)),
    )
    return pl.pallas_call(
        copy_block,
        grid_spec=grid_spec,
        out_shape=jax.ShapeDtypeStruct((fsdp * tp, rows, cols), full.dtype),
    )(slot_of, full)


def dot(a, b):
    return lax.dot_general(a, b, (((1,), (0,)), ((), ())), preferred_element_type=F32)


def dot_nt(a, b):
    return lax.dot_general(a, b, (((1,), (1,)), ((), ())), preferred_element_type=F32)


def dot_tn(a, b):
    return lax.dot_general(a, b, (((0,), (0,)), ((), ())), preferred_element_type=F32)


def norm_forward(values):
    average = jnp.mean(values, axis=-1, keepdims=True)
    centered = values - average
    inverse = lax.rsqrt(jnp.mean(centered * centered, axis=-1, keepdims=True) + 1e-12)
    return centered * inverse, inverse


def norm_backward(upstream, normal, inverse, gain):
    scaled = upstream * gain
    return inverse * (
        scaled
        - jnp.mean(scaled, axis=-1, keepdims=True)
        - normal * jnp.mean(scaled * normal, axis=-1, keepdims=True)
    )


def gelu_parts(x):
    below = 0.5 + 0.5 * lax.erf(x * math.sqrt(0.5))
    return x * below, below + x * (jnp.exp(-0.5 * (x * x)) * (1.0 / math.sqrt(2.0 * math.pi)))


def column_sum(array):
    return jnp.sum(array, axis=0, keepdims=True)


def each(count, step):
    lax.fori_loop(0, count, lambda i, carry: (step(i), carry)[1], 0)


def assemble(half, place_ref, pieces, weight):
    rows = weight.shape[1] // CUTS
    per = pieces[0].shape[0]
    for at, piece in enumerate(pieces):

        def copy(slot, at=at, piece=piece):
            place = place_ref[(half * len(pieces) + at) * per + slot]
            i = place // CUTS
            cut = place - i * CUTS
            weight[i, pl.ds(pl.multiple_of(cut * rows, rows), rows), :] = piece[slot]

        each(per, copy)


def put_blocks(half, slot_ref, out_ref, i, value, cols=slice(None)):
    rows = value.shape[0] // CUTS
    for cut in range(CUTS):
        slot = slot_ref[half * out_ref.shape[0] + i * CUTS + cut]
        out_ref[slot, :rows, cols] = value[cut * rows : (cut + 1) * rows].astype(out_ref.dtype)


def attention_kernel(half, place_ref, turn_ref, tokens_ref, ids_row, ids_col, bias_ref, *rest):
    if half == 0:
        output_bias, *rest = rest
        *pieces, weight, qkv_ref, context_ref, exponent_ref, total_ref, acc, turned_ref, mask = rest
        acc[...] = tokens_ref[...].astype(F32) + output_bias[...]
        turned_ref[...] = tokens_ref[...].T
    else:
        acc_ref, gain, shift, *rest = rest
        *pieces, weight, qkv_ref, context_ref, exponent_ref, total_ref = rest[:-5]
        normal_ref, inverse_ref, low_ref, mask, acc = rest[-5:]
        acc[...] = acc_ref[...]
    cols = context_ref.shape[1]
    count = weight.shape[0]
    assemble(half, place_ref, pieces, weight)
    mask[...] = jnp.where(ids_col[...] == ids_row[...], 0.0, -1e30)

    def step(i):
        bias = bias_ref[turn_ref[half * count + i]]
        qkv = (dot(tokens_ref[...], weight[i, :, : 3 * cols]) + bias).astype(BF16)
        qkv_ref[i] = qkv
        contexts = []
        for h in range(cols // HD):
            queries, keys, values = (
                qkv[:, part * cols + h * HD : part * cols + (h + 1) * HD] for part in range(3)
            )
            scores = dot_nt(keys, queries * (HD**-0.5)) + mask[...]
            top = jnp.max(scores, axis=0, keepdims=True)
            exponent = jnp.exp(scores - top)
            total = 1.0 / jnp.sum(exponent, axis=0, keepdims=True)
            exponent = exponent.astype(BF16)
            exponent_ref[i, h] = exponent
            contexts.append((dot_tn(values, exponent) * total).astype(BF16))
            total_ref[i, h : h + 1] = total
        context = jnp.concatenate(contexts, axis=0)
        context_ref[i] = context
        acc[...] += dot_nt(context.T, weight[i, :, 3 * cols :])

    each(count, step)
    if half == 1:
        normal, inverse = norm_forward(acc[...])
        normal_ref[...] = normal
        inverse_ref[...] = inverse
        low_ref[...] = (normal * gain[...] + shift[...]).astype(BF16)


def up_kernel(place_ref, turn_ref, low_ref, bias_ref, *rest):
    *pieces, weight_first, active_first, slope_first, weight_second, active_second, slope_second = rest
    many = len(pieces) // 2
    up_half(0, place_ref, turn_ref, low_ref, bias_ref, pieces[:many], weight_first, active_first, slope_first)
    up_half(1, place_ref, turn_ref, low_ref, bias_ref, pieces[many:], weight_second, active_second, slope_second)


def up_half(half, place_ref, turn_ref, low_ref, bias_ref, pieces, weight, active_ref, slope_ref):
    count = weight.shape[0]
    assemble(half, place_ref, pieces, weight)

    def step(i):
        pre = dot(low_ref[...], weight[i]) + bias_ref[turn_ref[half * count + i]]
        active, slope = gelu_parts(pre)
        active_ref[i] = active.astype(BF16)
        slope_ref[i] = slope.astype(BF16)

    each(count, step)


def down_first_kernel(place_ref, active_ref, normal_ref, first_gain, first_shift, bias_ref, *rest):
    *pieces, weight, acc = rest
    assemble(0, place_ref, pieces, weight)
    acc[...] = normal_ref[...] * first_gain[...] + (first_shift[...] + bias_ref[...])

    def step(i):
        acc[...] += dot_nt(active_ref[i], weight[i])

    each(weight.shape[0], step)


def down_second_kernel(place_ref, slot_ref, active_ref, acc_ref, gain, shift, cotangent_ref, *rest):
    *pieces, weight, output_ref, grad_ref, low_ref, turned_ref, sums_ref, send_ref, acc = rest
    count = weight.shape[0]
    assemble(1, place_ref, pieces, weight)
    acc[...] = acc_ref[...]

    def step(i):
        acc[...] += dot_nt(active_ref[i], weight[i])

    each(count, step)
    normal, inverse = norm_forward(acc[...])
    output_ref[...] = normal * gain[...] + shift[...]
    upstream = cotangent_ref[...].astype(F32)
    grad = norm_backward(upstream, normal, inverse, gain[...])
    grad_ref[...] = grad
    low = grad.astype(BF16)
    low_ref[...] = low
    turned_ref[...] = low.T
    sums_ref[0:1] = column_sum(grad)
    sums_ref[1:2] = column_sum(upstream * normal)
    sums_ref[2:3] = column_sum(upstream)
    each(count, lambda i: put_blocks(1, slot_ref, send_ref, i, dot(turned_ref[...], active_ref[i])))


def down_third_kernel(slot_ref, active_ref, turned_ref, keep_ref):
    each(
        active_ref.shape[0],
        lambda i: put_blocks(0, slot_ref, keep_ref, i, dot(turned_ref[...], active_ref[i])),
    )


def middle_kernel(half, slot_ref, low_grad_ref, slope_ref, *rest):
    if half == 1:
        grad_ref, low_ref, up_w, down_w, out_ref, sums_ref, acc, turned = rest
        acc[...] = grad_ref[...]
        turned[...] = low_ref[...].T
    else:
        acc_ref, turned, normal_ref, inverse_ref, gain, up_w, down_w, *rest = rest
        out_ref, sums_ref, resid_ref, resid_low_ref, resid_turned_ref, acc = rest
        acc[...] = acc_ref[...]

    def step(i):
        wide = dot(low_grad_ref[...], down_w[i]) * slope_ref[i].astype(F32)
        pre_grad = wide.astype(BF16)
        sums_ref[pl.ds(3 + i, 1)] = column_sum(wide)
        put_blocks(half, slot_ref, out_ref, i, dot(turned[...], pre_grad))
        acc[...] += dot_nt(pre_grad, up_w[i])

    each(up_w.shape[0], step)
    if half == 0:
        grad_one = acc[...]
        normal = normal_ref[...]
        resid = norm_backward(grad_one, normal, inverse_ref[...], gain[...])
        resid_ref[...] = resid
        low = resid.astype(BF16)
        resid_low_ref[...] = low
        resid_turned_ref[...] = low.T
        sums_ref[0:1] = column_sum(resid)
        sums_ref[1:2] = column_sum(grad_one * normal)
        sums_ref[2:3] = column_sum(grad_one)


def attention_back_kernel(slot_ref, turned_ref, resid_ref, resid_low_ref, resid_turned_ref, *rest):
    *parts, grad_ref, sums_second, sums_first, send_ref, keep_ref, grads_ref = rest
    grad_ref[...] = resid_ref[...]
    many = len(parts) // 2
    shared = (slot_ref, turned_ref, resid_low_ref, resid_turned_ref, grad_ref, grads_ref)
    attention_back(1, *shared, *parts[:many], sums_second, send_ref)
    attention_back(0, *shared, *parts[many:], sums_first, keep_ref)


def attention_back(
    half, slot_ref, turned_ref, resid_low_ref, resid_turned_ref, grad_ref, grads_ref, sums_in_ref, qkv_ref, context_ref,
    exponent_ref, total_ref, weight, sums_ref, out_ref,
):
    cols = context_ref.shape[1]
    factor = HD**-0.5
    extra = sums_ref.shape[1]
    main = out_ref.shape[1] - 2 * extra

    def step(i):
        outer = dot(resid_low_ref[...], weight[i, :, 3 * cols :])
        totals = total_ref[i].T
        query_grads, key_grads, value_grads = [], [], []
        for h in range(cols // HD):
            at = slice(h * HD, (h + 1) * HD)
            queries, keys, values = (
                qkv_ref[i, :, part * cols + h * HD : part * cols + (h + 1) * HD] for part in range(3)
            )
            queries = queries * factor
            upstream = (outer[:, at] * totals[:, h : h + 1]).astype(BF16)
            row_term = jnp.sum(
                upstream.T.astype(F32) * context_ref[i, at].astype(F32), axis=0, keepdims=True
            )
            exponent = exponent_ref[i, h]
            prob_grad = dot_nt(values, upstream)
            score_grad = (exponent.astype(F32) * (prob_grad - row_term)).astype(BF16)
            key_grads.append(dot(score_grad, queries).astype(BF16))
            value_grads.append(dot(exponent, upstream).astype(BF16))
            query_grads.append((dot_tn(keys, score_grad) * factor).astype(BF16))
        queries = jnp.concatenate(query_grads, axis=0).T
        grads_ref[i] = jnp.concatenate([queries, *key_grads, *value_grads], axis=1)

    each(weight.shape[0], step)
    count = weight.shape[0]
    grad = jnp.concatenate([grads_ref[i] for i in range(count)], axis=1)
    grad_ref[...] += dot_nt(grad, jnp.concatenate([weight[i, :, : 3 * cols] for i in range(count)], axis=1))
    weight_grad = dot(turned_ref[...], grad)
    out_grad = dot_nt(resid_turned_ref[...], jnp.concatenate([context_ref[i] for i in range(count)], axis=0))
    columns = column_sum(grad.astype(F32))
    for i in range(count):
        put_blocks(half, slot_ref, out_ref, i, weight_grad[:, 3 * cols * i : 3 * cols * (i + 1)], slice(0, 3 * cols))
        put_blocks(half, slot_ref, out_ref, i, out_grad[:, cols * i : cols * (i + 1)], slice(3 * cols, None))
        side = jnp.concatenate([columns[:, 3 * cols * i : 3 * cols * (i + 1)], jnp.zeros((1, cols), F32)], axis=1)
        side = jnp.concatenate([sums_in_ref[i], side], axis=0)
        sums_ref[i] = side
        high = side.astype(BF16)
        low = (side - high.astype(F32)).astype(BF16)
        side = jnp.concatenate([high, low], axis=0)
        for cut in range(CUTS):
            out_ref[slot_ref[half * out_ref.shape[0] + i * CUTS + cut], main:, :] = side


def unpack_kernel(keep_ref, moved_ref, query_ref, key_ref, value_ref, out_ref, side_ref):
    total = keep_ref[0].astype(F32) + moved_ref[0].astype(F32)
    rows, cols = query_ref.shape
    extra = side_ref.shape[0]
    for i, ref in enumerate((query_ref, key_ref, value_ref)):
        ref[...] = total[:rows, i * cols : (i + 1) * cols]
    out_ref[...] = total[:rows, 3 * cols :].T
    side_ref[...] = total[rows : rows + extra] + total[rows + extra :]


def call(kernel, pieces, scalars, inputs, outs, scratch, flops, limit=16):
    whole = pl.BlockSpec(memory_space=pltpu.VMEM)
    smem = pl.BlockSpec(memory_space=pltpu.SMEM)
    return pl.pallas_call(
        kernel,
        in_specs=[smem] * len(scalars) + [whole] * len(inputs) + [whole] * len(pieces),
        out_specs=[whole] * len(outs),
        out_shape=[jax.ShapeDtypeStruct(*out) for out in outs],
        scratch_shapes=scratch,
        compiler_params=pltpu.CompilerParams(vmem_limit_bytes=limit * MIB),
        cost_estimate=pl.CostEstimate(flops=1024, bytes_accessed=1024, transcendentals=0),
    )(*scalars, *inputs, *pieces)


def shards(
    steps,
    sources,
    fsdp,
    tp,
    tokens,
    segment_ids,
    query_weight,
    key_weight,
    value_weight,
    query_bias,
    value_bias,
    output_weight,
    output_bias,
    first_gain,
    first_shift,
    up_weight,
    up_bias,
    down_weight,
    down_bias,
    second_gain,
    second_shift,
    cotangent,
):
    rows, cols = query_weight.shape
    width = rows * fsdp
    units = up_weight.shape[1]
    count = fsdp * tp
    cut_rows = width // CUTS
    blocks_n = CUTS * tp
    direct = blocks_n == count
    place = lax.axis_index("tp")
    me = lax.axis_index("fsdp") * tp + place
    doc_ids = lax.dynamic_slice_in_dim(segment_ids, place * SEQ, SEQ)

    def mine(table):
        return lax.dynamic_index_in_dim(jnp.asarray(table, jnp.int32), me, keepdims=False)

    slot_of = mine(np.argsort(sources, axis=1))
    kept = tp // 2
    if direct:
        sides = np.array(sources).reshape(count, 2, -1) % tp
        columns = np.sort(np.array([[np.unique(part) for part in parts] for parts in sides]), axis=2)
        inner = (sides[..., None] == columns[:, :, None, :]).argmax(axis=-1)
        spots = inner * CUTS + np.array(sources).reshape(count, 2, -1) // tp
        places = mine(spots.reshape(count, -1))
        slots = mine(np.argsort(spots, axis=2).reshape(count, -1))
        turns = mine(columns.reshape(count, -1))
    else:
        places = slots = jnp.tile(jnp.arange(blocks_n // 2, dtype=jnp.int32), 2)
        turns = jnp.arange(tp, dtype=jnp.int32)

    def ready(pieces):
        if direct:
            return pieces
        full = laid_out(jnp.concatenate(pieces, axis=0), slot_of, fsdp, tp)
        full = full.reshape(CUTS, cut_rows, tp, -1).transpose(2, 0, 1, 3)
        full = full.reshape(2, blocks_n // 2, cut_rows, -1)
        return [full[0], full[1]]

    def outgoing(keep, send, extra=0):
        if direct:
            return Sum(keep, send, steps, extra)
        blocks = jnp.concatenate([keep, send], axis=0)[:, :cut_rows]
        full = blocks.reshape(tp, CUTS, cut_rows, -1).transpose(1, 2, 0, 3)
        blocks = cut_up(full.reshape(fsdp, rows, -1), slot_of, fsdp, tp)
        return Sum(blocks[: count // 2], blocks[count // 2 :], steps)

    query_bias, value_bias = query_bias.reshape(tp, 1, cols), value_bias.reshape(tp, 1, cols)
    blank = jnp.zeros_like(query_bias)
    qkv_bias = jnp.concatenate([query_bias, blank, value_bias], axis=2)
    up_bias = up_bias.reshape(tp, 1, units)
    vectors = jnp.stack(
        [output_bias, first_gain, first_shift, down_bias, second_gain, second_shift]
    ).reshape(6, 1, width)
    output_bias, first_gain, first_shift, down_bias, second_gain, second_shift = (
        vectors[i] for i in range(6)
    )
    ids_row, ids_col = doc_ids.reshape(1, -1), doc_ids.reshape(-1, 1)

    a = Gather(jnp.concatenate([query_weight, key_weight, value_weight, output_weight.T], axis=1), steps)
    b = Gather(up_weight, steps)
    c = Gather(down_weight.T, steps)
    if direct:
        pair = Gather(jnp.stack([up_weight, down_weight.T]), steps)
        first = a.step()
        pair.held = after(pair.held, first)
        a_x = a.step(qkv_bias, up_bias, vectors, ids_row, ids_col)
        pair.step()
        a.held, pair.held = lax.optimization_barrier((a.held, pair.held))
        a.step()
        pair.step()
        a.held, pair.held = lax.optimization_barrier((a.held, pair.held))
        b, c = pair.split()
        a_x = a.step(places, slots, turns)
        b_z = b.step()
        a.pieces, b.held = lax.optimization_barrier((a.pieces, b.held))
        attn_w = ready(a.finish())
        b_x = b.step()
        c2 = c.held
        c_z = swap(after(c2, b_z), steps[2])
        c_x = swap(after(c2, b_z), steps[3])
    else:
        for package in (a, b, c):
            for _ in steps[:-1]:
                package.step()
        attn_w = ready(a.finish())
    many = len(attn_w) // 2
    parts = kept
    weight = ((parts, width, units), BF16)
    half = ((blocks_n // 2, cut_rows, units), BF16)
    side_half = ((blocks_n // 2, cut_rows + 16, units), BF16)
    state = pltpu.VMEM((SEQ, width), F32)
    turned = pltpu.VMEM((width, SEQ), BF16)
    mask = pltpu.VMEM((SEQ, SEQ), F32)
    wide, narrow = (SEQ, width), ((SEQ, width), BF16)
    full = (wide, F32)
    flipped = ((width, SEQ), BF16)
    flops = 2 * SEQ * width * width
    kept_outs = [weight, ((parts, SEQ, 3 * cols), BF16), ((parts, cols, SEQ), BF16),
                 ((parts, cols // HD, SEQ, SEQ), BF16), ((parts, 8, SEQ), F32)]
    common = (tokens, ids_row, ids_col, qkv_bias)
    *attn_first, acc, tokens_turned = call(
        partial(attention_kernel, 0), attn_w[:many], (places, turns), (*common, output_bias),
        [*kept_outs, full, flipped], [mask], 4 * flops,
    )
    *attn_second, normal, inverse, low = call(
        partial(attention_kernel, 1), attn_w[many:], (places, turns), (*common, acc, first_gain, first_shift),
        [*kept_outs, full, ((SEQ, 1), F32), narrow], [mask, state], 4 * flops,
    )
    if direct:
        up_w = b.finish(inverse, b_x)
        c_xz = swap(after(c_z, inverse, c_x), steps[3])
    else:
        up_w = ready(b.finish())
    outs = [weight, ((parts, SEQ, units), BF16), ((parts, SEQ, units), BF16)]
    up_first, active_first, slope_first, up_second, active_second, slope_second = call(
        up_kernel, up_w, (places, turns), (low, up_bias), outs * 2, [], 6 * flops
    )
    if direct:
        down_w = [after(piece, slope_second, c_xz) for piece in (c2, c_z, c_x, c_xz)]
        down_w = [c2, c_z, c_x, c_xz] + [swap(piece, steps[4]) for piece in down_w]
    else:
        down_w = ready(c.finish())
    down_first, acc = call(
        down_first_kernel, down_w[: len(down_w) // 2], (places,),
        (active_first, normal, first_gain, first_shift, down_bias), [weight, full], [], 2 * flops,
    )
    down_second, layer_output, grad_two, grad_low, grad_turned, down_sums, down_send = call(
        down_second_kernel, down_w[len(down_w) // 2 :], (places, slots),
        (active_second, acc, second_gain, second_shift, cotangent),
        [weight, full, full, narrow, flipped, ((8, width), F32), half], [state], 5 * flops,
    )
    (down_keep,) = call(
        down_third_kernel, [], (slots,), (active_first, grad_turned), [half], [], 2 * flops
    )
    down_sum = outgoing(down_keep, down_send)
    if direct:
        first = down_sum.step()
        down_sum.start()
        grad_low = after(grad_low, first)
    up_send, sums_second, acc, low_turned = call(
        partial(middle_kernel, 1), [up_second, down_second], (slots,),
        (grad_low, slope_second, grad_two, low), [half, ((8, width), F32), full, flipped], [], 6 * flops,
    )
    up_keep, sums_first, resid, resid_low, resid_turned = call(
        partial(middle_kernel, 0), [up_first, down_first], (slots,),
        (grad_low, slope_first, acc, low_turned, normal, inverse, first_gain),
        [half, ((8, width), F32), full, narrow, flipped], [state], 6 * flops,
    )
    up_sum = outgoing(up_keep, up_send)
    if direct:
        moved = down_sum.moved
        sent = down_sum.end()
        down_sum.start(sums_first)
        up_sum.start()
        up_sum.hold(resid_low, sent)
        first = up_sum.end()
        up_sum.start()
        resid_low = after(resid_low, first, sent)
    shared = jnp.concatenate([down_sums[:3], sums_first[:3]], axis=0)[None]

    def with_units(sums):
        return jnp.concatenate([jnp.broadcast_to(shared, (parts, 6, width)), sums[3 : 3 + parts, None]], axis=1)

    weight_second, *attn_second = attn_second
    weight_first, *attn_first = attn_first
    side_sums = ((parts, 8, units), F32)
    input_grad, side_second, side_first, attn_send, attn_keep = call(
        attention_back_kernel, [], (slots,),
        (tokens_turned, resid, resid_low, resid_turned, with_units(sums_second), *attn_second, weight_second,
         with_units(sums_first), *attn_first, weight_first),
        [full, side_sums, side_sums, side_half, side_half], [pltpu.VMEM((parts, SEQ, 3 * cols), BF16)], 20 * flops,
    )
    attn_sum = outgoing(attn_keep, attn_send, 8)
    if direct:
        attn_sum.start(*down_sum.moved, *up_sum.moved)
        down_sum.end()
        up_sum.end()
        keep, moved = attn_sum.keep, attn_sum.moved
        part = keep.shape[0] // 4
        last = swap(attn_sum.add(keep[3 * part :], moved[1][part:]).astype(BF16), steps[3])
        up_sum.start()
        third = attn_sum.add(keep[2 * part : 3 * part], moved[1][:part]).astype(BF16)
        third = swap(after(third, last), steps[3])
        second = attn_sum.add(keep[part : 2 * part], moved[0][part:]).astype(BF16)
        attn_sum.moved = [swap(attn_sum.add(second, last).astype(BF16), steps[2])]
        first = attn_sum.add(keep[:part], moved[0][:part]).astype(BF16)
        attn_sum.keep, attn_sum.at = attn_sum.add(first, third).astype(BF16), 2
        up_sum.hold(last)
        up_sum.end()
        pair = Sum.merge(down_sum, up_sum)
        pair.start(third)
        both(attn_sum, pair)
        attn_sum.start()
        pair.start()
        attn_sum.end()
        attn_sum.start()
        pair.hold(*attn_sum.moved)
        finals = [[part] for part in pair.end()[0]]
    else:
        side = jnp.concatenate([side_first, side_second], axis=0)
        finals = []
        for package in (down_sum, up_sum, attn_sum):
            while package.at > 0:
                package.step()
            package.start()
            finals.append(package.end())
    if direct:
        small = ((rows, cols), F32)
        query_grad, key_grad, value_grad, out_grad, side = call(
            unpack_kernel, [], (), (attn_sum.keep, *attn_sum.moved),
            [small, small, small, ((cols, rows), F32), ((8, width), F32)], [], 1,
        )
    else:
        attn_grad = finals[2][0]
        query_grad, key_grad, value_grad = (attn_grad[:, i * cols : (i + 1) * cols] for i in range(3))
        out_grad = attn_grad[:, 3 * cols :].T
        side = lax.dynamic_index_in_dim(lax.psum(side, AXES), place, keepdims=False)
    return (
        layer_output,
        input_grad,
        query_grad,
        key_grad,
        value_grad,
        side[7, :cols],
        side[7, 2 * cols : 3 * cols],
        out_grad,
        side[3],
        side[4],
        side[5],
        finals[1][0],
        side[6],
        finals[0][0].T,
        side[0],
        side[1],
        side[2],
    )


def solution(mesh):
    fsdp, tp = mesh.shape["fsdp"], mesh.shape["tp"]
    steps, sources = exchange_plan(fsdp, tp)
    both, up, down = P(AXES, None), P("fsdp", "tp"), P("tp", "fsdp")
    return jax.shard_map(
        partial(shards, steps, sources, fsdp, tp),
        mesh=mesh,
        in_specs=(
            both, P("fsdp"), up, up, up, P(), P(), down, P(), P(), P(), up, P(), down, P(), P(), P(), both,
        ),
        out_specs=(
            both, both, up, up, up, P("tp"), P("tp"), down, P(), P(), P(), up, P("tp"), down, P(), P(), P(),
        ),
        check_vma=False,
    )
```
